32 devices in a mesh: grp: 2 (over x), rows: 8 (over z, core), cols: 2 (over y).
Axes of the slice: x: 2, y: 2, z: 4, core: 2. Of those that a mesh axis runs over, the one named last changes fastest.
Arguments:
- band_vectors: float32 [49152, 1024], P('rows'), may hold values from -6 to 6
- coulomb: float32 [49152], P('rows'), may hold values from 0.1 to 10
- pair_weight: float32 [1536], replicated, may hold values from 0.25 to 4
- occ_index: int32 [1536], replicated, may hold values from 0 to 255
- vir_index: int32 [1536], replicated, may hold values from 256 to 1023
- freq_index: int32 [1024], replicated, may hold values from 0 to 15
- freq_table: float32 [16], replicated, may hold values from 0.3 to 3
Outputs:
- self_energy: float32 [1024, 1024], P(('rows', 'cols'), 'grp')
The draws below stay inside these ranges and needn't reach their ends.
Inputs may be any that keep to these rules, and one draw needn't show every extreme that they name: `occ_index`: every pair's occupied band lies below 256. `vir_index`: every pair's empty band lies at 256 or above.
All inputs are finite; a program needn't handle non-finite values.
Results may differ from the reference program's by a relative error of at most 0.0001.
Values sent between devices are 32-bit elements; how exact they have to be, the bound alone decides.
No kernel may reach another device: no remote copies, remote signals or barrier semaphores. Data moves between devices by JAX's collectives and lax.ppermute only.
A program may use at most 192 MiB of HBM per device.

```python
import math
import jax
import jax.numpy as jnp
from jax import lax

NB = 49152
NBAND = 1024
NPAIR = 1536
NFREQ = 16
NOCC = 256
WIN = 1024
N_ROWS = 8


def plant(array, stream_key, least, high):
    spot = [jax.random.randint(jax.random.fold_in(stream_key, axis), (), 0, length) for axis, length in enumerate(array.shape)]
    longest = array.shape.index(max(array.shape))
    neighbour = spot[:longest] + [(spot[longest] + 1) % array.shape[longest]] + spot[longest + 1:]
    return array.at[tuple(spot)].set(least).at[tuple(neighbour)].set(high)


def level_of(rng, dims, cuts, least, top_value):
    factor_of = 1.0
    for dim, parts in cuts:
        steps = jax.random.uniform(jax.random.fold_in(jax.random.fold_in(rng, 6), dim), (parts,), jnp.float32, least / len(cuts), top_value / len(cuts))
        factor_of = factor_of * jnp.repeat(jnp.exp(steps), dims[dim] // parts).reshape((-1,) + (1,) * (len(dims) - 1 - dim))
    return factor_of


def normal_values(own_key, dims, spread, limit, shards=(), kind=jnp.bfloat16):
    array = jax.random.normal(own_key, dims, jnp.float32) * spread
    if len(shards) > 0:
        array = level_of(own_key, dims, shards, -0.22, 0.18) * array
    return jnp.clip(array, min=-limit, max=limit).astype(kind)


def setup_inputs(seed: int = 0) -> dict:
    seeds = jax.random.split(jax.random.key(seed), 8)
    return {
        "band_vectors": normal_values(seeds[0], (NB, NBAND), 1.0, 6.0, ((0, 8),), jnp.float32),
        "coulomb": jnp.clip(jnp.exp(math.log(10.0) - 4.6051702 * jax.random.uniform(seeds[1], (NB,), jnp.float32) ** level_of(seeds[1], (NB,), ((0, 8),), -0.2, 0.2)), 0.1, 10.0),
        "pair_weight": jnp.clip(jnp.exp(jax.random.uniform(seeds[2], (NPAIR,), jnp.float32, math.log(0.25), math.log(4.0))), 0.25, 4.0),
        "occ_index": plant(jax.random.randint(seeds[3], (NPAIR,), 0, NOCC), jax.random.fold_in(seeds[3], 1), 0, NOCC - 1).astype(jnp.int32),
        "vir_index": plant(jax.random.randint(seeds[4], (NPAIR,), NOCC, NBAND), jax.random.fold_in(seeds[4], 1), NOCC, NBAND - 1).astype(jnp.int32),
        "freq_index": plant(jax.random.randint(seeds[5], (NBAND,), 0, NFREQ), jax.random.fold_in(seeds[5], 1), 0, NFREQ - 1).astype(jnp.int32),
        "freq_table": jnp.clip(jnp.exp(jax.random.uniform(seeds[6], (NFREQ,), jnp.float32, math.log(0.3), math.log(3.0))), 0.3, 3.0),
    }


def reference(band_vectors, coulomb, pair_weight, occ_index, vir_index, freq_index, freq_table):
    highest = lax.Precision.HIGHEST
    row_block = NB // N_ROWS
    band_weight = freq_table[freq_index]

    def accumulate(totals, offset):
        response, coupling = totals
        block_rows = lax.dynamic_slice_in_dim(band_vectors, offset, row_block, 0)
        coul_rows = lax.dynamic_slice_in_dim(coulomb, offset, row_block, 0)
        pair_cols = block_rows[:, occ_index] * block_rows[:, vir_index] * pair_weight[None, :]
        weighted = pair_cols[:, :WIN] * coul_rows[:, None]
        response = response + lax.dot_general(pair_cols, weighted, (((0,), (0,)), ((), ())), precision=highest, preferred_element_type=jnp.float32)
        band_cols = block_rows * coul_rows[:, None] * band_weight[None, :]
        coupling = coupling + lax.dot_general(band_cols, pair_cols, (((0,), (0,)), ((), ())), precision=highest, preferred_element_type=jnp.float32)
        return ((response, coupling), None)
    offsets = (jnp.arange(N_ROWS) * row_block).astype(jnp.int32)
    initial = (jnp.zeros((NPAIR, WIN), jnp.float32), jnp.zeros((NBAND, NPAIR), jnp.float32))
    (response, coupling), unused = lax.scan(accumulate, initial, offsets)
    response = response * (1.0 / NB)
    coupling = coupling * (1.0 / math.sqrt(NB))
    mixed_rows = jnp.dot(coupling, response, precision=highest, preferred_element_type=jnp.float32)
    self_energy = lax.dot_general(mixed_rows, coupling[:, :WIN], (((1,), (1,)), ((), ())), precision=highest, preferred_element_type=jnp.float32)
    return self_energy * (1.0 / math.sqrt(WIN))
```

```python
import math

import jax
import jax.numpy as jnp
from jax import lax
from jax.experimental import pallas as pl
from jax.experimental.pallas import tpu as pltpu
from jax.sharding import PartitionSpec as P

PANEL = 512
LANES = 128
PAIR_BLOCK = 256
GATHER_BLOCK = 128
VMEM_BYTES = 60 * 2**20


def split(value):
    high = value.astype(jnp.bfloat16)
    return high, (value - high.astype(jnp.float32)).astype(jnp.bfloat16)


def three_pass(left_high, left_low, right_high, right_low):
    def dot(left, right):
        return jnp.dot(left, right, preferred_element_type=jnp.float32)

    return dot(left_high, right_high) + (dot(left_low, right_high) + dot(left_high, right_low))


def coupling_kernel(
    block_ref, occ_ref, vir_ref, occ_own_ref, vir_own_ref, coulomb_ref, band_ref,
    high_ref, low_ref, coupling_ref, own_high_ref, own_low_ref,
    turned, products, band_high, band_low, incoming, arrived,
):
    step = pl.program_id(0)
    bands = band_ref.shape[1]
    basis_rows = band_ref.shape[0]
    groups = basis_rows // LANES
    stride = turned.shape[0] // bands
    piece = incoming.shape[1]
    width = band_high.shape[1]
    pieces = basis_rows // piece
    batch = products.shape[0] // stride

    def gather(occ, vir, first):
        @pl.loop(0, batch, unroll=4)
        def _(pair):
            left = occ[first + pair] * stride
            right = vir[first + pair] * stride
            products[pl.ds(pair * stride, groups), :] = (
                turned[pl.ds(left, groups), :] * turned[pl.ds(right, groups), :]
            )

    def weight(group):
        return coulomb_ref[group : group + 1, :]

    @pl.when(step == 0)
    def _():
        def fetch(index):
            return pltpu.make_async_copy(
                band_ref.at[pl.ds(index * piece, piece), :],
                incoming.at[index % 2],
                arrived.at[index % 2],
            )

        own_bands = pl.ds(pl.multiple_of(block_ref[0] * width, LANES), width)
        fetch(0).start()
        for index in range(pieces):
            if index + 1 < pieces:
                fetch(index + 1).start()
            fetch(index).wait()
            for part in range(piece // LANES):
                group = index * (piece // LANES) + part
                rows = pl.ds(part * LANES, LANES)
                turned[pl.ds(group, bands, stride=stride), :] = incoming[index % 2, rows, :].T
                column = jnp.broadcast_to(weight(group), (LANES, LANES)).T
                own = incoming[index % 2, rows, own_bands]
                own = own * jnp.concatenate([column] * (width // LANES), axis=1)
                here = pl.ds(group * LANES, LANES)
                band_high[here, :], band_low[here, :] = split(own)
        for first in range(0, own_high_ref.shape[1], batch):
            gather(occ_own_ref, vir_own_ref, first)
            for group in range(groups):
                own = products[pl.ds(group, batch, stride=stride), :] * weight(group)
                here = pl.ds(group * LANES, LANES)
                there = pl.ds(first, batch)
                own_high_ref[here, there], own_low_ref[here, there] = split(own.T)

    for first in range(0, high_ref.shape[0], batch):
        gather(occ_ref, vir_ref, step * high_ref.shape[0] + first)
        for group in range(groups):
            here = pl.ds(first, batch)
            there = pl.ds(group * LANES, LANES)
            high_ref[here, there], low_ref[here, there] = split(
                products[pl.ds(group, batch, stride=stride), :]
            )
    coupling_ref[...] = three_pass(high_ref[...], low_ref[...], band_high[...], band_low[...])


def pair_coupling(band_vectors, coulomb, occ, vir, occ_own, vir_own, block, width):
    basis_rows, bands = band_vectors.shape
    pairs = occ.shape[0]
    own = occ_own.shape[0]
    groups = basis_rows // LANES
    stride = groups + 1 - groups % 2
    piece = min(256, basis_rows)
    scalars = pl.BlockSpec(memory_space=pltpu.SMEM)
    whole = pl.BlockSpec((basis_rows, own), lambda i: (0, 0), pipeline_mode=pl.Buffered(1))
    rows = pl.BlockSpec((PAIR_BLOCK, basis_rows), lambda i: (i, 0))
    half = jnp.bfloat16
    return pl.pallas_call(
        coupling_kernel,
        grid=(pairs // PAIR_BLOCK,),
        in_specs=[scalars] * 5
        + [pl.BlockSpec((groups, LANES), lambda i: (0, 0)), pl.BlockSpec(memory_space=pl.ANY)],
        out_specs=[rows, rows, pl.BlockSpec((PAIR_BLOCK, width), lambda i: (i, 0)), whole, whole],
        out_shape=[
            jax.ShapeDtypeStruct((pairs, basis_rows), half),
            jax.ShapeDtypeStruct((pairs, basis_rows), half),
            jax.ShapeDtypeStruct((pairs, width), jnp.float32),
            jax.ShapeDtypeStruct((basis_rows, own), half),
            jax.ShapeDtypeStruct((basis_rows, own), half),
        ],
        scratch_shapes=[
            pltpu.VMEM((bands * stride, LANES), jnp.float32),
            pltpu.VMEM((GATHER_BLOCK * stride, LANES), jnp.float32),
            pltpu.VMEM((basis_rows, width), half),
            pltpu.VMEM((basis_rows, width), half),
            pltpu.VMEM((2, piece, bands), jnp.float32),
            pltpu.SemaphoreType.DMA((2,)),
        ],
        compiler_params=pltpu.CompilerParams(vmem_limit_bytes=VMEM_BYTES),
        cost_estimate=pl.CostEstimate(
            flops=6 * basis_rows * pairs * width,
            bytes_accessed=4 * basis_rows * (bands + pairs),
            transcendentals=0,
        ),
        name="coupling",
    )(
        block, occ, vir, occ_own, vir_own, coulomb.reshape(groups, LANES), band_vectors
    )


def response_kernel(high_ref, low_ref, own_high_ref, own_low_ref, response_ref):
    response_ref[...] = three_pass(
        high_ref[...], low_ref[...], own_high_ref[...], own_low_ref[...]
    )


def pair_response(high, low, own_high, own_low):
    pairs, basis_rows = high.shape
    own = own_high.shape[1]
    rows = pl.BlockSpec((PAIR_BLOCK, basis_rows), lambda i: (i, 0))
    whole = pl.BlockSpec((basis_rows, own), lambda i: (0, 0))
    return pl.pallas_call(
        response_kernel,
        grid=(pairs // PAIR_BLOCK,),
        in_specs=[rows, rows, whole, whole],
        out_specs=pl.BlockSpec((PAIR_BLOCK, own), lambda i: (i, 0)),
        out_shape=jax.ShapeDtypeStruct((pairs, own), jnp.float32),
        compiler_params=pltpu.CompilerParams(vmem_limit_bytes=VMEM_BYTES),
        cost_estimate=pl.CostEstimate(
            flops=6 * basis_rows * pairs * own,
            bytes_accessed=4 * basis_rows * (own + pairs),
            transcendentals=0,
        ),
        name="response",
    )(high, low, own_high, own_low)


def per_device(band_vectors, coulomb, pair_weight, occ_index, vir_index, freq_index, freq_table):
    row_count = lax.axis_size("rows")
    col_count = lax.axis_size("cols")
    group_count = lax.axis_size("grp")
    blocks = col_count * group_count
    lines = row_count // 2
    row = lax.axis_index("rows")
    core, line = lax.rem(row, 2), lax.div(row, 2)
    column = lax.axis_index("cols")
    group = lax.axis_index("grp")
    block = group * col_count + column
    basis_rows, bands = band_vectors.shape
    pairs = occ_index.shape[0]
    window = PANEL * group_count
    basis = basis_rows * row_count

    def ordered(values):
        def shares(part):
            return part.reshape(lines, 2, -1).swapaxes(0, 1)

        return jnp.concatenate([shares(values[:window]), shares(values[window:])], axis=2)

    def own_window(values):
        return lax.dynamic_index_in_dim(
            values[:window].reshape(row_count, blocks, -1), block, 1, keepdims=False
        ).reshape(-1)

    def pick(values, index, axis=0):
        return lax.dynamic_index_in_dim(values, index, axis, keepdims=False)

    other_core = [(i, i ^ 1) for i in range(row_count)]

    def shift(step):
        return [(i, (i // 2 + step) % lines * 2 + i % 2) for i in range(row_count)]

    def scatter_rows(values):
        received = lax.ppermute(pick(values, 1 - core), "rows", other_core)
        both = pick(values, core) + received
        total = pick(both, line)
        arrived = [
            lax.ppermute(pick(both, lax.rem(line + step, lines)), "rows", shift(step))
            for step in range(1, lines)
        ]
        for value in arrived:
            total = total + value
        return total

    def gather_blocks(values):
        across = [(i, i ^ 1) for i in range(col_count)]
        pair = jnp.stack([values, lax.ppermute(values, "cols", across)])
        pair = jnp.where(column == 0, pair, pair[::-1])
        across = [(i, i ^ 1) for i in range(group_count)]
        quad = jnp.stack([pair, lax.ppermute(pair, "grp", across)])
        quad = jnp.where(group == 0, quad, quad[::-1])
        return quad.reshape((blocks,) + values.shape)

    occ_own, vir_own = own_window(occ_index), own_window(vir_index)
    high, low, partial_coupling, own_high, own_low = pair_coupling(
        band_vectors, coulomb, ordered(occ_index).reshape(-1), ordered(vir_index).reshape(-1),
        occ_own, vir_own, block.reshape(1), bands // blocks,
    )
    partial_response = pair_response(high, low, own_high, own_low)

    share = pairs // row_count
    shaped = (2, lines, share, -1)
    weights = ordered(pair_weight)
    own_weights = pick(pick(weights, core), line)
    coupling = scatter_rows(partial_coupling.reshape(shaped))
    coupling = coupling * (own_weights[:, None] * (1.0 / math.sqrt(basis)))
    all_coupling = gather_blocks(coupling)
    all_coupling = all_coupling.swapaxes(0, 1).reshape(share, bands)
    sub = window // (row_count * blocks)
    part = lax.dynamic_slice_in_dim(all_coupling, block * sub, sub, 0)
    parts = [part] + [lax.ppermute(part, "rows", shift(step)) for step in range(1, lines)]
    parts = jnp.stack(parts)
    beside = lax.ppermute(parts, "rows", other_core)
    both = jnp.where(core == 0, jnp.stack([parts, beside], 1), jnp.stack([beside, parts], 1))
    both = jnp.roll(both[::-1], line + 1, axis=0)
    window_coupling = both.reshape(row_count * sub, bands)

    response = scatter_rows(partial_response.reshape(shaped))
    response = response * (
        own_weights[:, None] * own_window(pair_weight)[None, :] * (1.0 / basis)
    )
    matches = freq_index[:, None] == jnp.arange(freq_table.shape[0], dtype=jnp.int32)[None, :]
    band_weight = jnp.sum(jnp.where(matches, freq_table[None, :], 0.0), axis=1)
    mixed = lax.dot_general(
        all_coupling, response, (((0,), (0,)), ((), ())),
        precision=lax.Precision.HIGH, preferred_element_type=jnp.float32,
    )
    mixed = scatter_rows(mixed.reshape(lines, 2, bands // row_count, -1).swapaxes(0, 1))
    energy = lax.dot_general(
        mixed, window_coupling, (((1,), (0,)), ((), ())),
        precision=lax.Precision.HIGH, preferred_element_type=jnp.float32,
    )
    here = bands // row_count
    own_band_weight = lax.dynamic_slice_in_dim(band_weight, row * here, here, 0)
    energy = energy * (
        own_band_weight[:, None] * band_weight[None, :] * (1.0 / math.sqrt(window))
    )
    energy = energy.reshape(col_count, here // col_count, group_count, bands // group_count)
    across = [(i, i ^ 1) for i in range(col_count)]
    received = lax.ppermute(pick(energy, 1 - column), "cols", across)
    energy = pick(energy, column) + received
    across = [(i, i ^ 1) for i in range(group_count)]
    received = lax.ppermute(pick(energy, 1 - group, 1), "grp", across)
    return pick(energy, group, 1) + received


def solution(mesh):
    placed = (P("rows", None), P("rows"), P(), P(), P(), P(), P())
    return jax.shard_map(
        per_device,
        mesh=mesh,
        in_specs=placed,
        out_specs=P(("rows", "cols"), "grp"),
        check_vma=False,
    )
```

```python
import functools
import math

import jax
import jax.numpy as jnp
from jax import lax
from jax.experimental import pallas as pl
from jax.experimental.pallas import tpu as pltpu
from jax.sharding import PartitionSpec as P

PANEL = 512
LANES = 128
CHUNK = 1024
VMEM_BYTES = 60 * 2**20
PARTS = 2
SLICES = 4


def split(value):
    high = value.astype(jnp.bfloat16)
    return high, (value - high.astype(jnp.float32)).astype(jnp.bfloat16)


def three_pass(left_high, left_low, right_high, right_low):
    def dot(left, right):
        return jnp.dot(left, right, preferred_element_type=jnp.float32)

    return dot(left_high, right_high) + (dot(left_low, right_high) + dot(left_high, right_low))


def product_kernel(
    paired, occ_ref, vir_ref, occ_own_ref, vir_own_ref, coulomb_ref, band_ref, out_ref,
    incoming, arrived, turned_even, turned_odd, products,
    left_high_even, left_high_odd, left_low_even, left_low_odd,
    right_high_even, right_high_odd, right_low_even, right_low_odd,
):
    turned = turned_even, turned_odd
    left_high, left_low = (left_high_even, left_high_odd), (left_low_even, left_low_odd)
    right_high, right_low = (right_high_even, right_high_odd), (right_low_even, right_low_odd)
    chunk, bands = incoming.shape[1:]
    chunks = band_ref.shape[0] // chunk
    groups = chunk // LANES
    stride = turned_even.shape[0] // bands
    pairs = out_ref.shape[0] // PARTS
    own = out_ref.shape[1] // PARTS
    depth = chunk // PARTS

    def fetch(c):
        slot = lax.rem(c, 3)
        return pltpu.make_async_copy(
            band_ref.at[pl.ds(c * chunk, chunk), :], incoming.at[slot], arrived.at[slot]
        )

    def turn(c, k, parity, part):
        group = k * (groups // PARTS) + part
        rows = pl.ds(pl.multiple_of(group * LANES, LANES), LANES)
        turned[parity][pl.ds(group, bands, stride=stride), :] = (
            incoming[lax.rem(c, 3), rows, :].T
        )

    def gather(parity, occ, vir, first, count, place):
        for pair in range(count):
            left = turned[parity][pl.ds(occ[first + pair], groups), :]
            right = turned[parity][pl.ds(vir[first + pair], groups), :]
            products[pl.ds((place + pair) * stride, groups), :] = left * right

    def weight(c, group):
        return coulomb_ref[pl.ds(lax.rem(c, chunks) * groups + group, 1), :]

    def prepare_own(c, k, parity):
        gather(parity, occ_own_ref, vir_own_ref, k * own, own, pairs)
        for group in range(groups):
            value = products[pl.ds(pairs * stride + group, own, stride=stride), :]
            here = pl.ds(group * LANES, LANES)
            there = pl.ds(pl.multiple_of(k * own, own), own)
            right_high[parity][here, there], right_low[parity][here, there] = split(
                (value * weight(c, group)).T
            )

    def prepare_bands(c, k, parity, part):
        here = pl.ds(pl.multiple_of(k * depth + part * LANES, LANES), LANES)
        right_high[parity][here, :], right_low[parity][here, :] = split(
            incoming[lax.rem(c, 3), here, :]
        )

    def prepare(c, k, parity, first, count):
        gather(parity, occ_ref, vir_ref, k * pairs + first, count, first)
        for group in range(groups):
            value = products[pl.ds(first * stride + group, count, stride=stride), :]
            if not paired:
                value = value * weight(c, group)
            here = pl.ds(pl.multiple_of(k * pairs + first, 16), count)
            there = pl.ds(group * LANES, LANES)
            left_high[parity][here, there], left_low[parity][here, there] = split(value)

    def multiply(k, parity, rows, columns):
        here = pl.ds(pl.multiple_of(k * depth, depth), depth)
        out_ref[rows, columns] += three_pass(
            left_high[parity][rows, here], left_low[parity][rows, here],
            right_high[parity][here, columns], right_low[parity][here, columns],
        )

    def body(c, k, parity, first, second, third):
        turns = groups // PARTS if third else 0
        for part in range(max(SLICES, turns)):
            if first and part < SLICES:
                if paired:
                    height = out_ref.shape[0] // SLICES
                    multiply(k, parity, pl.ds(part * height, height), slice(None))
                else:
                    height = out_ref.shape[1] // SLICES
                    multiply(k, parity, slice(None), pl.ds(part * height, height))
            if part < turns:
                turn(c + 2, k, parity, part)
            if second:
                if paired and part == 0:
                    prepare_own(c + 1, k, 1 - parity)
                if not paired and part < depth // LANES:
                    prepare_bands(c + 1, k, 1 - parity, part)
                if part < SLICES:
                    count = pairs // SLICES
                    prepare(c + 1, k, 1 - parity, part * count, count)

    for c in range(min(3, chunks)):
        fetch(c).start()
    out_ref[...] = jnp.zeros_like(out_ref)
    fetch(0).wait()

    @pl.loop(0, PARTS)
    def _(k):
        body(-2, k, 0, False, False, True)

    if chunks > 1:
        fetch(1).wait()

    @pl.loop(0, PARTS)
    def _(k):
        body(-1, k, 1, False, True, True)

    def advance(c, parity):
        @pl.when(c + 2 < chunks)
        def _():
            fetch(c + 2).wait()

        @pl.when(c + 3 < chunks)
        def _():
            fetch(c + 3).start()

        @pl.loop(0, PARTS)
        def _(k):
            body(c, k, parity, True, True, True)

    @pl.loop(0, chunks // 2)
    def _(index):
        advance(2 * index, 0)
        advance(2 * index + 1, 1)

    if chunks % 2:
        advance(chunks - 1, 0)


def pair_product(band_vectors, coulomb, occ, vir, occ_own, vir_own, paired, name):
    basis_rows, bands = band_vectors.shape
    pairs = occ.shape[0]
    width = occ_own.shape[0] if paired else bands
    chunk = math.gcd(CHUNK, basis_rows)
    groups = chunk // LANES
    stride = groups + 1 - groups % 2
    half = jnp.bfloat16
    scalars = pl.BlockSpec(memory_space=pltpu.SMEM)
    whole = pl.BlockSpec(memory_space=pltpu.VMEM)
    batch = (pairs + (width if paired else 0)) // PARTS
    return pl.pallas_call(
        functools.partial(product_kernel, paired),
        in_specs=[scalars] * 4 + [whole, pl.BlockSpec(memory_space=pl.ANY)],
        out_specs=whole,
        out_shape=jax.ShapeDtypeStruct((pairs, width), jnp.float32),
        scratch_shapes=[
            pltpu.VMEM((3, chunk, bands), jnp.float32),
            pltpu.SemaphoreType.DMA((3,)),
            pltpu.VMEM((bands * stride, LANES), jnp.float32),
            pltpu.VMEM((bands * stride, LANES), jnp.float32),
            pltpu.VMEM((batch * stride, LANES), jnp.float32),
        ]
        + [pltpu.VMEM((pairs, chunk), half)] * 4
        + [pltpu.VMEM((chunk, width), half)] * 4,
        compiler_params=pltpu.CompilerParams(vmem_limit_bytes=VMEM_BYTES),
        cost_estimate=pl.CostEstimate(
            flops=6 * basis_rows * pairs * width,
            bytes_accessed=4 * basis_rows * bands,
            transcendentals=0,
        ),
        name=name,
    )(
        occ * stride, vir * stride, occ_own * stride, vir_own * stride,
        coulomb.reshape(basis_rows // LANES, LANES), band_vectors,
    )


def per_device(band_vectors, coulomb, pair_weight, occ_index, vir_index, freq_index, freq_table):
    row_count = lax.axis_size("rows")
    col_count = lax.axis_size("cols")
    group_count = lax.axis_size("grp")
    blocks = col_count * group_count
    lines = row_count // 2
    row = lax.axis_index("rows")
    core, line = lax.rem(row, 2), lax.div(row, 2)
    column = lax.axis_index("cols")
    group = lax.axis_index("grp")
    block = group * col_count + column
    basis_rows, bands = band_vectors.shape
    pairs = occ_index.shape[0]
    window = PANEL * group_count
    basis = basis_rows * row_count

    def ordered(values):
        def shares(part):
            return part.reshape(lines, 2, blocks, -1).swapaxes(0, 1)

        return jnp.concatenate([shares(values[:window]), shares(values[window:])], axis=3)

    def own_window(values):
        shaped = values[:window].reshape(row_count, blocks, -1)
        return pick(shaped, block, 1).reshape(-1)

    def pick(values, index, axis=0):
        return lax.dynamic_index_in_dim(values, index, axis, keepdims=False)

    other_core = [(i, i ^ 1) for i in range(row_count)]

    def shift(step):
        return [(i, (i // 2 + step) % lines * 2 + i % 2) for i in range(row_count)]

    def add_cores(values):
        received = lax.ppermute(pick(values, 1 - core), "rows", other_core)
        return pick(values, core) + received

    def scatter_lines(values):
        arrived = [
            lax.ppermute(pick(values, lax.rem(line + step, lines)), "rows", shift(step))
            for step in range(1, lines)
        ]
        total = pick(values, line)
        for value in arrived:
            total = total + value
        return total

    def gather_blocks(values):
        across = [(i, i ^ 1) for i in range(col_count)]
        pair = jnp.stack([values, lax.ppermute(values, "cols", across)])
        pair = jnp.where(column == 0, pair, pair[::-1])
        across = [(i, i ^ 1) for i in range(group_count)]
        quad = jnp.stack([pair, lax.ppermute(pair, "grp", across)])
        quad = jnp.where(group == 0, quad, quad[::-1])
        return quad.reshape((blocks,) + values.shape)

    occ_own, vir_own = own_window(occ_index), own_window(vir_index)
    occ, vir, weights = ordered(occ_index), ordered(vir_index), ordered(pair_weight)
    partial_coupling = pair_product(
        band_vectors, coulomb, pick(occ, block, 2).reshape(-1), pick(vir, block, 2).reshape(-1),
        occ_own, vir_own, False, "coupling",
    )
    share = pairs // row_count
    partial_coupling = add_cores(partial_coupling.reshape(2, lines, share // blocks, bands))
    partial_coupling, occ, vir = lax.optimization_barrier((partial_coupling, occ, vir))
    partial_response = pair_product(
        band_vectors, coulomb, occ.reshape(-1), vir.reshape(-1), occ_own, vir_own, True, "response"
    )

    partial_response = add_cores(partial_response.reshape(2, lines, share, window // blocks))
    own_weights = pick(pick(weights, core), line)
    coupling = scatter_lines(partial_coupling)
    partial_response, coupling = lax.optimization_barrier((partial_response, coupling))
    coupling = coupling * (pick(own_weights, block)[:, None] * (1.0 / math.sqrt(basis)))
    all_coupling = gather_blocks(coupling).reshape(share, bands)
    response = scatter_lines(partial_response)
    response = response * (
        own_weights.reshape(-1)[:, None] * own_window(pair_weight)[None, :] * (1.0 / basis)
    )
    sub = window // (row_count * blocks)
    response, part = lax.optimization_barrier((response, coupling[:sub]))
    parts = [part] + [lax.ppermute(part, "rows", shift(step)) for step in range(1, lines)]
    parts = jnp.stack(parts)
    beside = lax.ppermute(parts, "rows", other_core)
    both = jnp.where(core == 0, jnp.stack([parts, beside], 1), jnp.stack([beside, parts], 1))
    both = jnp.roll(both[::-1], line + 1, axis=0)
    window_coupling = both.reshape(row_count * sub, bands)

    matches = freq_index[:, None] == jnp.arange(freq_table.shape[0], dtype=jnp.int32)[None, :]
    band_weight = jnp.sum(jnp.where(matches, freq_table[None, :], 0.0), axis=1)
    mixed = lax.dot_general(
        all_coupling, response, (((0,), (0,)), ((), ())),
        precision=lax.Precision.HIGH, preferred_element_type=jnp.float32,
    )
    mixed = add_cores(mixed.reshape(lines, 2, bands // row_count, -1).swapaxes(0, 1))
    mixed = scatter_lines(mixed)
    energy = lax.dot_general(
        mixed, window_coupling, (((1,), (0,)), ((), ())),
        precision=lax.Precision.HIGH, preferred_element_type=jnp.float32,
    )
    here = bands // row_count
    own_band_weight = lax.dynamic_slice_in_dim(band_weight, row * here, here, 0)
    energy = energy * (
        own_band_weight[:, None] * band_weight[None, :] * (1.0 / math.sqrt(window))
    )
    energy = energy.reshape(col_count, here // col_count, group_count, bands // group_count)
    across = [(i, i ^ 1) for i in range(col_count)]
    received = lax.ppermute(pick(energy, 1 - column), "cols", across)
    energy = pick(energy, column) + received
    across = [(i, i ^ 1) for i in range(group_count)]
    received = lax.ppermute(pick(energy, 1 - group, 1), "grp", across)
    return pick(energy, group, 1) + received


def solution(mesh):
    placed = (P("rows", None), P("rows"), P(), P(), P(), P(), P())
    return jax.shard_map(
        per_device,
        mesh=mesh,
        in_specs=placed,
        out_specs=P(("rows", "cols"), "grp"),
        check_vma=False,
    )
```

```python
import functools
import math

import jax
import jax.numpy as jnp
from jax import lax
from jax.experimental import pallas as pl
from jax.experimental.pallas import tpu as pltpu
from jax.sharding import PartitionSpec as P

PANEL = 512
LANES = 128
CHUNK = 1024
SLICES = 4
PAIR_SLICES = 8
VMEM_BYTES = 60 * 2**20


def split(value):
    high = value.astype(jnp.bfloat16)
    return high, (value - high.astype(jnp.float32)).astype(jnp.bfloat16)


def three_pass(left_high, left_low, right_high, right_low):
    def dot(left, right):
        return jnp.dot(left, right, preferred_element_type=jnp.float32)

    return dot(left_high, right_high) + (dot(left_low, right_high) + dot(left_high, right_low))


def pair_position(place, lines, blocks, window, pairs):
    inside, outside = window // (2 * lines * blocks), (pairs - window) // (2 * lines * blocks)
    rest, place = divmod(place, inside + outside)
    rest, block = divmod(rest, blocks)
    core, line = divmod(rest, lines)
    share = (line * 2 + core) * blocks + block
    if place < inside:
        return share * inside + place, inside
    return window + share * outside + place - inside, outside


def coupling_kernel(
    shape, block_ref, occ_ref, vir_ref, coulomb_ref, band_ref, out_ref, turned_ref,
    incoming, arrived, turned_even, turned_odd, handed, products,
    left_high_even, left_high_odd, left_low_even, left_low_odd, right_high, right_low,
):
    turned = turned_even, turned_odd
    left_high, left_low = (left_high_even, left_high_odd), (left_low_even, left_low_odd)
    chunk, bands = incoming.shape[1:]
    chunks = band_ref.shape[0] // chunk
    groups = chunk // LANES
    stride = products.shape[0] // out_ref.shape[0]
    pairs = out_ref.shape[0]
    lines, blocks, window = shape
    count = pairs // SLICES
    width = bands // SLICES
    block = block_ref[0]

    def fetch(c):
        slot = lax.rem(c, 3)
        return pltpu.make_async_copy(
            band_ref.at[pl.ds(c * chunk, chunk), :], incoming.at[slot], arrived.at[slot]
        )

    def hand_on(c, parity):
        return pltpu.make_async_copy(turned[parity], turned_ref.at[c], handed.at[parity])

    def turn(c, parity, part):
        flat = turned[parity].reshape(bands * groups, LANES)
        for group in range(part, groups, SLICES):
            rows = pl.ds(group * LANES, LANES)
            flat[pl.ds(group, bands, stride=groups), :] = incoming[lax.rem(c, 3), rows, :].T

    def prepare(c, parity, part):
        here = pl.ds(part * width, width)
        right_high[:, here], right_low[:, here] = split(incoming[lax.rem(c, 3), :, here])
        for pair in range(part * count, part * count + count):
            per_share = pairs // (2 * lines)
            share, place = divmod(pair, per_share)
            index, step = pair_position(
                share * per_share * blocks + place, lines, blocks, window, occ_ref.shape[0]
            )
            index = index + block * step
            products[pl.ds(pair * stride, groups), :] = (
                turned[parity][occ_ref[index]] * turned[parity][vir_ref[index]]
            )
        for group in range(groups):
            weight = coulomb_ref[pl.ds(lax.rem(c, chunks) * groups + group, 1), :]
            value = products[pl.ds(part * count * stride + group, count, stride=stride), :]
            here = pl.ds(part * count, count)
            there = pl.ds(group * LANES, LANES)
            left_high[parity][here, there], left_low[parity][here, there] = split(value * weight)

    def multiply(parity, part):
        here = pl.ds(part * width, width)
        out_ref[:, here] += three_pass(
            left_high[parity][...], left_low[parity][...], right_high[:, here], right_low[:, here]
        )

    for c in range(min(3, chunks)):
        fetch(c).start()
    out_ref[...] = jnp.zeros_like(out_ref)
    fetch(0).wait()
    for part in range(SLICES):
        turn(0, 0, part)
    hand_on(0, 0).start()
    if chunks > 1:
        fetch(1).wait()
    for part in range(SLICES):
        if chunks > 1:
            turn(1, 1, part)
        prepare(0, 0, part)
    if chunks > 1:
        hand_on(1, 1).start()

    def advance(c, parity):
        @pl.when(c + 2 < chunks)
        def _():
            fetch(c + 2).wait()

        @pl.when(c + 3 < chunks)
        def _():
            fetch(c + 3).start()

        hand_on(c, parity).wait()
        for part in range(SLICES):
            multiply(parity, part)
            turn(c + 2, parity, part)
            prepare(c + 1, 1 - parity, part)

        @pl.when(c + 2 < chunks)
        def _():
            hand_on(c + 2, parity).start()

    @pl.loop(0, chunks // 2)
    def _(index):
        advance(2 * index, 0)
        advance(2 * index + 1, 1)

    if chunks % 2:
        advance(chunks - 1, 0)


def pair_coupling(band_vectors, coulomb, occ, vir, block, shape):
    basis_rows, bands = band_vectors.shape
    lines, blocks, window = shape
    pairs = occ.shape[0] // blocks
    chunk = math.gcd(CHUNK, basis_rows)
    groups = chunk // LANES
    stride = groups + 1 - groups % 2
    half = jnp.bfloat16
    scalars = pl.BlockSpec(memory_space=pltpu.SMEM)
    whole = pl.BlockSpec(memory_space=pltpu.VMEM)
    outside = pl.BlockSpec(memory_space=pl.ANY)
    return pl.pallas_call(
        functools.partial(coupling_kernel, shape),
        in_specs=[scalars] * 3 + [whole, outside],
        out_specs=[whole, outside],
        out_shape=[
            jax.ShapeDtypeStruct((pairs, bands), jnp.float32),
            jax.ShapeDtypeStruct((basis_rows // chunk, bands, groups, LANES), jnp.float32),
        ],
        scratch_shapes=[
            pltpu.VMEM((3, chunk, bands), jnp.float32),
            pltpu.SemaphoreType.DMA((3,)),
            pltpu.VMEM((bands, groups, LANES), jnp.float32),
            pltpu.VMEM((bands, groups, LANES), jnp.float32),
            pltpu.SemaphoreType.DMA((2,)),
            pltpu.VMEM((pairs * stride, LANES), jnp.float32),
        ]
        + [pltpu.VMEM((pairs, chunk), half)] * 4
        + [pltpu.VMEM((chunk, bands), half)] * 2,
        compiler_params=pltpu.CompilerParams(vmem_limit_bytes=VMEM_BYTES),
        cost_estimate=pl.CostEstimate(
            flops=6 * basis_rows * pairs * bands,
            bytes_accessed=8 * basis_rows * bands,
            transcendentals=0,
        ),
        name="coupling",
    )(block, occ, vir, coulomb.reshape(basis_rows // LANES, LANES), band_vectors)


def response_kernel(
    shape, block_ref, occ_ref, vir_ref, coulomb_ref, turned_ref, out_ref,
    turned, arrived, products, left_high_even, left_high_odd, left_low_even, left_low_odd,
    right_high, right_low,
):
    left_high, left_low = (left_high_even, left_high_odd), (left_low_even, left_low_odd)
    chunks, bands, groups, _ = turned_ref.shape
    pairs, own = out_ref.shape
    lines, blocks, window = shape
    height = left_high_even.shape[0]
    slices = pairs // height
    every = chunks * groups
    block = block_ref[0]
    inside, outside = window // (2 * lines * blocks), (pairs - window) // (2 * lines * blocks)
    half_slices = slices // 2
    per_slice = lines // half_slices

    def fetch(c):
        here = pl.ds(pl.multiple_of(c * groups, groups), groups)
        return pltpu.make_async_copy(turned_ref.at[c], turned.at[:, here, :], arrived.at[c])

    def gather(index, place, here, stride):
        products[pl.ds(place * stride, here.size), :] = (
            turned[occ_ref[index], here, :] * turned[vir_ref[index], here, :]
        )

    def gather_slice(i, here, stride):
        first = (lax.rem(i, half_slices) * (per_slice * 2) + lax.div(i, half_slices)) * blocks
        for pair in range(height):
            share, place = divmod(pair, blocks * (inside + outside))
            part, place = divmod(place, inside + outside)
            index = share * 2 * blocks + part
            if place < inside:
                index = first * inside + (index * inside + place)
            else:
                index = first * outside + (window + index * outside + place - inside)
            gather(index, pair, here, stride)

    def split_slice(parity, base, count, stride):
        for group in range(count):
            there = pl.ds(base + group * LANES, LANES)
            left_high[parity][:, there], left_low[parity][:, there] = split(
                products[pl.ds(group, height, stride=stride), :]
            )

    def multiply(i, parity):
        here = pl.ds(pl.multiple_of(i * height, height), height)
        out_ref[here, :] = three_pass(
            left_high[parity][...], left_low[parity][...], right_high[...], right_low[...]
        )

    for c in range(chunks):
        fetch(c).start()

    @pl.loop(0, chunks)
    def _(c):
        fetch(c).wait()
        here = pl.ds(pl.multiple_of(c * groups, groups), groups)
        base = pl.multiple_of(c * (groups * LANES), LANES)
        stride = groups + 1 - groups % 2
        for pair in range(own):
            share, place = divmod(pair, inside)
            gather(block * inside + (share * blocks * inside + place), pair, here, stride)
        for group in range(groups):
            weight = coulomb_ref[pl.ds(c * groups + group, 1), :]
            value = products[pl.ds(group, own, stride=stride), :] * weight
            there = pl.ds(base + group * LANES, LANES)
            right_high[there, :], right_low[there, :] = split(value.T)
        gather_slice(0, here, stride)
        split_slice(0, base, groups, stride)

    stride = every + 1 - every % 2

    @pl.loop(0, slices // 2)
    def _(index):
        for parity in range(2):
            multiply(2 * index + parity, parity)
            after = jnp.minimum(2 * index + parity + 1, slices - 1)
            gather_slice(after, pl.ds(0, every), stride)
            split_slice(1 - parity, 0, every, stride)


def pair_response(turned, coulomb, occ, vir, block, shape):
    steps, bands, groups, _ = turned.shape
    lines, blocks, window = shape
    pairs = occ.shape[0]
    own = window // blocks
    every = steps * groups
    basis_rows = every * LANES
    height = pairs // PAIR_SLICES
    places = max(height * (every + 1 - every % 2), own * (groups + 1 - groups % 2))
    half = jnp.bfloat16
    scalars = pl.BlockSpec(memory_space=pltpu.SMEM)
    whole = pl.BlockSpec(memory_space=pltpu.VMEM)
    return pl.pallas_call(
        functools.partial(response_kernel, shape),
        in_specs=[scalars] * 3 + [whole, pl.BlockSpec(memory_space=pl.ANY)],
        out_specs=whole,
        out_shape=jax.ShapeDtypeStruct((pairs, own), jnp.float32),
        scratch_shapes=[
            pltpu.VMEM((bands, every, LANES), jnp.float32),
            pltpu.SemaphoreType.DMA((steps,)),
            pltpu.VMEM((places, LANES), jnp.float32),
        ]
        + [pltpu.VMEM((height, basis_rows), half)] * 4
        + [pltpu.VMEM((basis_rows, own), half)] * 2,
        compiler_params=pltpu.CompilerParams(vmem_limit_bytes=VMEM_BYTES),
        cost_estimate=pl.CostEstimate(
            flops=6 * basis_rows * pairs * own,
            bytes_accessed=4 * basis_rows * bands,
            transcendentals=0,
        ),
        name="response",
    )(block, occ, vir, coulomb.reshape(basis_rows // LANES, LANES), turned)


def per_device(band_vectors, coulomb, pair_weight, occ_index, vir_index, freq_index, freq_table):
    row_count = lax.axis_size("rows")
    col_count = lax.axis_size("cols")
    group_count = lax.axis_size("grp")
    blocks = col_count * group_count
    lines = row_count // 2
    row = lax.axis_index("rows")
    core, line = lax.rem(row, 2), lax.div(row, 2)
    column = lax.axis_index("cols")
    group = lax.axis_index("grp")
    block = group * col_count + column
    basis_rows, bands = band_vectors.shape
    pairs = occ_index.shape[0]
    window = PANEL * group_count
    basis = basis_rows * row_count

    def ordered(values):
        def shares(part):
            return part.reshape(lines, 2, blocks, -1).swapaxes(0, 1)

        return jnp.concatenate([shares(values[:window]), shares(values[window:])], axis=3)

    def own_window(values):
        shaped = values[:window].reshape(row_count, blocks, -1)
        return pick(shaped, block, 1).reshape(-1)

    def pick(values, index, axis=0):
        return lax.dynamic_index_in_dim(values, index, axis, keepdims=False)

    other_core = [(i, i ^ 1) for i in range(row_count)]

    def shift(step):
        return [(i, (i // 2 + step) % lines * 2 + i % 2) for i in range(row_count)]

    def add_cores(values):
        received = lax.ppermute(pick(values, 1 - core), "rows", other_core)
        return pick(values, core) + received

    def scatter_lines(values):
        arrived = [
            lax.ppermute(pick(values, lax.rem(line + step, lines)), "rows", shift(step))
            for step in range(1, lines)
        ]
        total = pick(values, line)
        for value in arrived:
            total = total + value
        return total

    def gather_blocks(values):
        across = [(i, i ^ 1) for i in range(col_count)]
        pair = jnp.stack([values, lax.ppermute(values, "cols", across)])
        pair = jnp.where(column == 0, pair, pair[::-1])
        across = [(i, i ^ 1) for i in range(group_count)]
        quad = jnp.stack([pair, lax.ppermute(pair, "grp", across)])
        quad = jnp.where(group == 0, quad, quad[::-1])
        return quad.reshape((blocks,) + values.shape)

    weights = ordered(pair_weight)
    shape = (lines, blocks, window)
    place = block.reshape(1)
    partial_coupling, turned = pair_coupling(
        band_vectors, coulomb, occ_index, vir_index, place, shape
    )
    share = pairs // row_count
    partial_coupling = add_cores(partial_coupling.reshape(2, lines, share // blocks, bands))
    partial_coupling, turned = lax.optimization_barrier((partial_coupling, turned))
    partial_response = pair_response(turned, coulomb, occ_index, vir_index, place, shape)
    coupling = scatter_lines(partial_coupling)
    partial_response, coupling = lax.optimization_barrier((partial_response, coupling))
    partial_response = add_cores(partial_response.reshape(2, lines, share, window // blocks))
    partial_response, coupling = lax.optimization_barrier((partial_response, coupling))
    own_weights = pick(pick(weights, core), line)
    coupling = coupling * (pick(own_weights, block)[:, None] * (1.0 / math.sqrt(basis)))
    all_coupling = gather_blocks(coupling).reshape(share, bands)
    response = scatter_lines(partial_response)
    response = response * (
        own_weights.reshape(-1)[:, None] * own_window(pair_weight)[None, :] * (1.0 / basis)
    )
    sub = window // (row_count * blocks)
    response, part = lax.optimization_barrier((response, coupling[:sub]))
    parts = [part] + [lax.ppermute(part, "rows", shift(step)) for step in range(1, lines)]
    parts = jnp.stack(parts)
    beside = lax.ppermute(parts, "rows", other_core)
    both = jnp.where(core == 0, jnp.stack([parts, beside], 1), jnp.stack([beside, parts], 1))
    both = jnp.roll(both[::-1], line + 1, axis=0)
    window_coupling = both.reshape(row_count * sub, bands)

    matches = freq_index[:, None] == jnp.arange(freq_table.shape[0], dtype=jnp.int32)[None, :]
    band_weight = jnp.sum(jnp.where(matches, freq_table[None, :], 0.0), axis=1)
    mixed = lax.dot_general(
        all_coupling, response, (((0,), (0,)), ((), ())),
        precision=lax.Precision.HIGH, preferred_element_type=jnp.float32,
    )
    mixed = add_cores(mixed.reshape(lines, 2, bands // row_count, -1).swapaxes(0, 1))
    mixed = scatter_lines(mixed)
    energy = lax.dot_general(
        mixed, window_coupling, (((1,), (0,)), ((), ())),
        precision=lax.Precision.HIGH, preferred_element_type=jnp.float32,
    )
    here = bands // row_count
    own_band_weight = lax.dynamic_slice_in_dim(band_weight, row * here, here, 0)
    energy = energy * (
        own_band_weight[:, None] * band_weight[None, :] * (1.0 / math.sqrt(window))
    )
    energy = energy.reshape(col_count, here // col_count, group_count, bands // group_count)
    across = [(i, i ^ 1) for i in range(col_count)]
    received = lax.ppermute(pick(energy, 1 - column), "cols", across)
    energy = pick(energy, column) + received
    across = [(i, i ^ 1) for i in range(group_count)]
    received = lax.ppermute(pick(energy, 1 - group, 1), "grp", across)
    return pick(energy, group, 1) + received


def solution(mesh):
    placed = (P("rows", None), P("rows"), P(), P(), P(), P(), P())
    return jax.shard_map(
        per_device,
        mesh=mesh,
        in_specs=placed,
        out_specs=P(("rows", "cols"), "grp"),
        check_vma=False,
    )
```

```python
import functools
import math

import jax
import jax.numpy as jnp
from jax import lax
from jax.experimental import pallas as pl
from jax.experimental.pallas import tpu as pltpu
from jax.sharding import PartitionSpec as P

PANEL = 512
LANES = 128
CHUNK = 1024
SLICES = 4
PAIR_SLICES = 8
VMEM_BYTES = 60 * 2**20


def split(value):
    high = value.astype(jnp.bfloat16)
    return high, (value - high.astype(jnp.float32)).astype(jnp.bfloat16)


def three_pass(left_high, left_low, right_high, right_low):
    def dot(left, right):
        return jnp.dot(left, right, preferred_element_type=jnp.float32)

    return dot(left_high, right_high) + (dot(left_low, right_high) + dot(left_high, right_low))


def pair_position(place, lines, blocks, window, pairs):
    inside, outside = window // (2 * lines * blocks), (pairs - window) // (2 * lines * blocks)
    rest, place = divmod(place, inside + outside)
    rest, block = divmod(rest, blocks)
    core, line = divmod(rest, lines)
    share = (line * 2 + core) * blocks + block
    if place < inside:
        return share * inside + place, inside
    return window + share * outside + place - inside, outside


def coupling_kernel(
    shape, block_ref, occ_ref, vir_ref, coulomb_ref, band_ref, out_ref, turned_ref,
    incoming, arrived, turned_even, turned_odd, handed, products,
    left_high_even, left_high_odd, left_low_even, left_low_odd, right_high, right_low,
):
    turned = turned_even, turned_odd
    left_high, left_low = (left_high_even, left_high_odd), (left_low_even, left_low_odd)
    chunk, bands = incoming.shape[1:]
    chunks = band_ref.shape[0] // chunk
    groups = chunk // LANES
    stride = products.shape[0] // out_ref.shape[0]
    pairs = out_ref.shape[0]
    lines, blocks, window = shape
    count = pairs // SLICES
    width = bands // SLICES
    block = block_ref[0]

    def fetch(c):
        slot = lax.rem(c, 3)
        return pltpu.make_async_copy(
            band_ref.at[pl.ds(c * chunk, chunk), :], incoming.at[slot], arrived.at[slot]
        )

    def hand_on(c, parity):
        return pltpu.make_async_copy(turned[parity], turned_ref.at[c], handed.at[parity])

    def turn(c, parity, part):
        flat = turned[parity].reshape(bands * groups, LANES)
        for group in range(part, groups, SLICES):
            rows = pl.ds(group * LANES, LANES)
            flat[pl.ds(group, bands, stride=groups), :] = incoming[lax.rem(c, 3), rows, :].T

    def prepare(c, parity, part):
        here = pl.ds(part * width, width)
        right_high[:, here], right_low[:, here] = split(incoming[lax.rem(c, 3), :, here])
        for pair in range(part * count, part * count + count):
            per_share = pairs // (2 * lines)
            share, place = divmod(pair, per_share)
            index, step = pair_position(
                share * per_share * blocks + place, lines, blocks, window, occ_ref.shape[0]
            )
            index = index + block * step
            products[pl.ds(pair * stride, groups), :] = (
                turned[parity][occ_ref[index]] * turned[parity][vir_ref[index]]
            )
        for group in range(groups):
            weight = coulomb_ref[pl.ds(lax.rem(c, chunks) * groups + group, 1), :]
            value = products[pl.ds(part * count * stride + group, count, stride=stride), :]
            here = pl.ds(part * count, count)
            there = pl.ds(group * LANES, LANES)
            left_high[parity][here, there], left_low[parity][here, there] = split(value * weight)

    def multiply(parity, part):
        here = pl.ds(part * width, width)
        out_ref[:, here] += three_pass(
            left_high[parity][...], left_low[parity][...], right_high[:, here], right_low[:, here]
        )

    for c in range(min(3, chunks)):
        fetch(c).start()
    out_ref[...] = jnp.zeros_like(out_ref)
    fetch(0).wait()
    for part in range(SLICES):
        turn(0, 0, part)
    hand_on(0, 0).start()
    if chunks > 1:
        fetch(1).wait()
    for part in range(SLICES):
        if chunks > 1:
            turn(1, 1, part)
        prepare(0, 0, part)
    if chunks > 1:
        hand_on(1, 1).start()

    def advance(c, parity):
        @pl.when(c + 2 < chunks)
        def _():
            fetch(c + 2).wait()

        @pl.when(c + 3 < chunks)
        def _():
            fetch(c + 3).start()

        hand_on(c, parity).wait()
        for part in range(SLICES):
            multiply(parity, part)
            turn(c + 2, parity, part)
            prepare(c + 1, 1 - parity, part)

        @pl.when(c + 2 < chunks)
        def _():
            hand_on(c + 2, parity).start()

    @pl.loop(0, chunks // 2)
    def _(index):
        advance(2 * index, 0)
        advance(2 * index + 1, 1)

    if chunks % 2:
        advance(chunks - 1, 0)


def pair_coupling(band_vectors, coulomb, occ, vir, block, shape):
    basis_rows, bands = band_vectors.shape
    lines, blocks, window = shape
    pairs = occ.shape[0] // blocks
    chunk = math.gcd(CHUNK, basis_rows)
    groups = chunk // LANES
    stride = groups + 1 - groups % 2
    half = jnp.bfloat16
    scalars = pl.BlockSpec(memory_space=pltpu.SMEM)
    whole = pl.BlockSpec(memory_space=pltpu.VMEM)
    outside = pl.BlockSpec(memory_space=pl.ANY)
    return pl.pallas_call(
        functools.partial(coupling_kernel, shape),
        in_specs=[scalars] * 3 + [whole, outside],
        out_specs=[whole, outside],
        out_shape=[
            jax.ShapeDtypeStruct((pairs, bands), jnp.float32),
            jax.ShapeDtypeStruct((basis_rows // chunk, bands, groups, LANES), jnp.float32),
        ],
        scratch_shapes=[
            pltpu.VMEM((3, chunk, bands), jnp.float32),
            pltpu.SemaphoreType.DMA((3,)),
            pltpu.VMEM((bands, groups, LANES), jnp.float32),
            pltpu.VMEM((bands, groups, LANES), jnp.float32),
            pltpu.SemaphoreType.DMA((2,)),
            pltpu.VMEM((pairs * stride, LANES), jnp.float32),
        ]
        + [pltpu.VMEM((pairs, chunk), half)] * 4
        + [pltpu.VMEM((chunk, bands), half)] * 2,
        compiler_params=pltpu.CompilerParams(vmem_limit_bytes=VMEM_BYTES),
        cost_estimate=pl.CostEstimate(
            flops=6 * basis_rows * pairs * bands,
            bytes_accessed=8 * basis_rows * bands,
            transcendentals=0,
        ),
        name="coupling",
    )(block, occ, vir, coulomb.reshape(basis_rows // LANES, LANES), band_vectors)


def gather_kernel(
    shape, block_ref, occ_ref, vir_ref, coulomb_ref, turned_ref,
    high_ref, low_ref, own_high_ref, own_low_ref, turned, arrived, products,
):
    step = pl.program_id(0)
    chunks, bands, groups, _ = turned_ref.shape
    height = high_ref.shape[0]
    own = own_high_ref.shape[1]
    lines, blocks, window = shape
    every = chunks * groups
    block = block_ref[0]
    inside, outside = window // (2 * lines * blocks), occ_ref.shape[0] - window
    outside = outside // (2 * lines * blocks)
    half, core = lax.div(step, 4), lax.rem(lax.div(step, 2), 2)
    first = (lax.rem(step, 2) * lines + core) * blocks + half * (blocks // 2)

    def fetch(c):
        here = pl.ds(pl.multiple_of(c * groups, groups), groups)
        return pltpu.make_async_copy(turned_ref.at[c], turned.at[:, here, :], arrived.at[c])

    def gather(index, place, here, stride):
        products[pl.ds(place * stride, here.size), :] = (
            turned[occ_ref[index], here, :] * turned[vir_ref[index], here, :]
        )

    def gather_slice(here, stride):
        for pair in range(height):
            line, place = divmod(pair, blocks // 2 * (inside + outside))
            part, place = divmod(place, inside + outside)
            index = line * 2 * blocks + part
            if place < inside:
                index = first * inside + (index * inside + place)
            else:
                index = first * outside + (window + index * outside + place - inside)
            gather(index, pair, here, stride)

    def split_slice(base, count, stride):
        for group in range(count):
            there = pl.ds(base + group * LANES, LANES)
            high_ref[:, there], low_ref[:, there] = split(
                products[pl.ds(group, height, stride=stride), :]
            )

    @pl.when(step == 0)
    def _():
        for c in range(chunks):
            fetch(c).start()

        @pl.loop(0, chunks)
        def _(c):
            fetch(c).wait()
            here = pl.ds(pl.multiple_of(c * groups, groups), groups)
            base = pl.multiple_of(c * (groups * LANES), LANES)
            stride = groups + 1 - groups % 2
            for pair in range(own):
                share, place = divmod(pair, inside)
                gather(block * inside + (share * blocks * inside + place), pair, here, stride)
            for group in range(groups):
                weight = coulomb_ref[pl.ds(c * groups + group, 1), :]
                value = products[pl.ds(group, own, stride=stride), :] * weight
                there = pl.ds(base + group * LANES, LANES)
                own_high_ref[there, :], own_low_ref[there, :] = split(value.T)
            gather_slice(here, stride)
            split_slice(base, groups, stride)

    @pl.when(step > 0)
    def _():
        stride = every + 1 - every % 2
        gather_slice(pl.ds(0, every), stride)
        split_slice(0, every, stride)


def pair_products(turned, coulomb, occ, vir, block, shape):
    steps, bands, groups, _ = turned.shape
    lines, blocks, window = shape
    pairs = occ.shape[0]
    own = window // blocks
    every = steps * groups
    basis_rows = every * LANES
    height = pairs // PAIR_SLICES
    places = max(height * (every + 1 - every % 2), own * (groups + 1 - groups % 2))
    scalars = pl.BlockSpec(memory_space=pltpu.SMEM)
    rows = pl.BlockSpec((height, basis_rows), lambda i: (i, 0))
    whole = pl.BlockSpec((basis_rows, own), lambda i: (0, 0), pipeline_mode=pl.Buffered(1))
    return pl.pallas_call(
        functools.partial(gather_kernel, shape),
        grid=(PAIR_SLICES,),
        in_specs=[scalars] * 3
        + [pl.BlockSpec((every, LANES), lambda i: (0, 0)), pl.BlockSpec(memory_space=pl.ANY)],
        out_specs=[rows, rows, whole, whole],
        out_shape=[jax.ShapeDtypeStruct((pairs, basis_rows), jnp.bfloat16)] * 2
        + [jax.ShapeDtypeStruct((basis_rows, own), jnp.bfloat16)] * 2,
        scratch_shapes=[
            pltpu.VMEM((bands, every, LANES), jnp.float32),
            pltpu.SemaphoreType.DMA((steps,)),
            pltpu.VMEM((places, LANES), jnp.float32),
        ],
        compiler_params=pltpu.CompilerParams(vmem_limit_bytes=VMEM_BYTES),
        cost_estimate=pl.CostEstimate(
            flops=0,
            bytes_accessed=4 * basis_rows * (bands + pairs + own),
            transcendentals=0,
        ),
        name="products",
    )(block, occ, vir, coulomb.reshape(every, LANES), turned)


def response_kernel(high_ref, low_ref, own_high_ref, own_low_ref, out_ref):
    out_ref[...] = three_pass(high_ref[...], low_ref[...], own_high_ref[...], own_low_ref[...])


def pair_response(high, low, own_high, own_low, half):
    pairs, basis_rows = high.shape
    own = own_high.shape[1]
    height = pairs // PAIR_SLICES
    steps = PAIR_SLICES // 2
    rows = pl.BlockSpec((height, basis_rows), lambda i: (i + half * steps, 0))
    whole = pl.BlockSpec((basis_rows, own), lambda i: (0, 0), pipeline_mode=pl.Buffered(1))
    return pl.pallas_call(
        response_kernel,
        grid=(steps,),
        in_specs=[rows, rows, whole, whole],
        out_specs=pl.BlockSpec((height, own), lambda i: (i, 0)),
        out_shape=jax.ShapeDtypeStruct((pairs // 2, own), jnp.float32),
        compiler_params=pltpu.CompilerParams(vmem_limit_bytes=VMEM_BYTES),
        cost_estimate=pl.CostEstimate(
            flops=3 * basis_rows * pairs * own,
            bytes_accessed=2 * basis_rows * (pairs + 2 * own),
            transcendentals=0,
        ),
        name=f"response_{half}",
    )(high, low, own_high, own_low)


def per_device(band_vectors, coulomb, pair_weight, occ_index, vir_index, freq_index, freq_table):
    row_count = lax.axis_size("rows")
    col_count = lax.axis_size("cols")
    group_count = lax.axis_size("grp")
    blocks = col_count * group_count
    lines = row_count // 2
    row = lax.axis_index("rows")
    core, line = lax.rem(row, 2), lax.div(row, 2)
    column = lax.axis_index("cols")
    group = lax.axis_index("grp")
    block = group * col_count + column
    basis_rows, bands = band_vectors.shape
    pairs = occ_index.shape[0]
    window = PANEL * group_count
    basis = basis_rows * row_count

    def ordered(values):
        def shares(part):
            return part.reshape(lines, 2, blocks, -1).swapaxes(0, 1)

        return jnp.concatenate([shares(values[:window]), shares(values[window:])], axis=3)

    def own_window(values):
        shaped = values[:window].reshape(row_count, blocks, -1)
        return pick(shaped, block, 1).reshape(-1)

    def pick(values, index, axis=0):
        return lax.dynamic_index_in_dim(values, index, axis, keepdims=False)

    other_core = [(i, i ^ 1) for i in range(row_count)]

    def shift(step):
        return [(i, (i // 2 + step) % lines * 2 + i % 2) for i in range(row_count)]

    def add_cores(values):
        received = lax.ppermute(pick(values, 1 - core), "rows", other_core)
        return pick(values, core) + received

    def scatter_lines(values):
        arrived = [
            lax.ppermute(pick(values, lax.rem(line + step, lines)), "rows", shift(step))
            for step in range(1, lines)
        ]
        total = pick(values, line)
        for value in arrived:
            total = total + value
        return total

    def gather_blocks(values):
        across = [(i, i ^ 1) for i in range(col_count)]
        pair = jnp.stack([values, lax.ppermute(values, "cols", across)])
        pair = jnp.where(column == 0, pair, pair[::-1])
        across = [(i, i ^ 1) for i in range(group_count)]
        quad = jnp.stack([pair, lax.ppermute(pair, "grp", across)])
        quad = jnp.where(group == 0, quad, quad[::-1])
        return quad.reshape((blocks,) + values.shape)

    weights = ordered(pair_weight)
    shape = (lines, blocks, window)
    place = block.reshape(1)
    partial_coupling, turned = pair_coupling(
        band_vectors, coulomb, occ_index, vir_index, place, shape
    )
    share = pairs // row_count
    partial_coupling = add_cores(partial_coupling.reshape(2, lines, share // blocks, bands))
    partial_coupling, turned = lax.optimization_barrier((partial_coupling, turned))
    high, low, own_high, own_low = pair_products(
        turned, coulomb, occ_index, vir_index, place, shape
    )
    coupling = scatter_lines(partial_coupling)
    high, low, coupling = lax.optimization_barrier((high, low, coupling))

    own_weights = pick(pick(weights, core), line)
    coupling = coupling * (pick(own_weights, block)[:, None] * (1.0 / math.sqrt(basis)))
    all_coupling = gather_blocks(coupling).reshape(share, bands)
    sub = window // (row_count * blocks)
    part = coupling[:sub]
    parts = [part] + [lax.ppermute(part, "rows", shift(step)) for step in range(1, lines)]

    def sum_cores(values):
        return add_cores(values.reshape(2, lines, share // 2, window // blocks))

    first = pair_response(high, low, own_high, own_low, 0)
    first, all_coupling, *parts = lax.optimization_barrier((first, all_coupling, *parts))
    first = sum_cores(first)
    first, high = lax.optimization_barrier((first, high))
    second = pair_response(high, low, own_high, own_low, 1)
    first = scatter_lines(first)
    second, first = lax.optimization_barrier((second, first))
    second = scatter_lines(sum_cores(second))
    response = jnp.concatenate([first, second]) * (
        own_weights.reshape(-1)[:, None] * own_window(pair_weight)[None, :] * (1.0 / basis)
    )

    parts = jnp.stack(parts)
    beside = lax.ppermute(parts, "rows", other_core)
    both = jnp.where(core == 0, jnp.stack([parts, beside], 1), jnp.stack([beside, parts], 1))
    both = jnp.roll(both[::-1], line + 1, axis=0)
    window_coupling = both.reshape(row_count * sub, bands)
    matches = freq_index[:, None] == jnp.arange(freq_table.shape[0], dtype=jnp.int32)[None, :]
    band_weight = jnp.sum(jnp.where(matches, freq_table[None, :], 0.0), axis=1)
    mixed = lax.dot_general(
        all_coupling, response, (((0,), (0,)), ((), ())),
        precision=lax.Precision.HIGH, preferred_element_type=jnp.float32,
    )
    mixed = add_cores(mixed.reshape(lines, 2, bands // row_count, -1).swapaxes(0, 1))
    mixed = scatter_lines(mixed)
    energy = lax.dot_general(
        mixed, window_coupling, (((1,), (0,)), ((), ())),
        precision=lax.Precision.HIGH, preferred_element_type=jnp.float32,
    )
    here = bands // row_count
    own_band_weight = lax.dynamic_slice_in_dim(band_weight, row * here, here, 0)
    energy = energy * (
        own_band_weight[:, None] * band_weight[None, :] * (1.0 / math.sqrt(window))
    )
    energy = energy.reshape(col_count, here // col_count, group_count, bands // group_count)
    total = pick(pick(energy, column), group, 1)
    for step in range(1, blocks):
        there_group, there_column = divmod(step, col_count)
        away_group = lax.rem(group + there_group, group_count)
        away_column = lax.rem(column + there_column, col_count)
        targets = [
            (
                i,
                (i // col_count + there_group) % group_count * col_count
                + (i % col_count + there_column) % col_count,
            )
            for i in range(blocks)
        ]
        total = total + lax.ppermute(
            pick(pick(energy, away_column), away_group, 1), ("grp", "cols"), targets
        )
    return total


def solution(mesh):
    placed = (P("rows", None), P("rows"), P(), P(), P(), P(), P())
    return jax.shard_map(
        per_device,
        mesh=mesh,
        in_specs=placed,
        out_specs=P(("rows", "cols"), "grp"),
        check_vma=False,
    )
```

```python
import functools
import math

import jax
import jax.numpy as jnp
from jax import lax
from jax.experimental import pallas as pl
from jax.experimental.pallas import tpu as pltpu
from jax.sharding import PartitionSpec as P

PANEL = 512
LANES = 128
CHUNK = 1024
SLICES = 4
PAIR_SLICES = 8
PIECES = 6
VMEM_BYTES = 60 * 2**20


def split(value):
    high = value.astype(jnp.bfloat16)
    return high, (value - high.astype(jnp.float32)).astype(jnp.bfloat16)


def three_pass(left_high, left_low, right_high, right_low):
    def dot(left, right):
        return jnp.dot(left, right, preferred_element_type=jnp.float32)

    return dot(left_high, right_high) + (dot(left_low, right_high) + dot(left_high, right_low))


def pair_position(place, lines, blocks, window, pairs):
    inside, outside = window // (2 * lines * blocks), (pairs - window) // (2 * lines * blocks)
    rest, place = divmod(place, inside + outside)
    rest, block = divmod(rest, blocks)
    core, line = divmod(rest, lines)
    share = (line * 2 + core) * blocks + block
    if place < inside:
        return share * inside + place, inside
    return window + share * outside + place - inside, outside


def coupling_kernel(
    shape, block_ref, occ_ref, vir_ref, coulomb_ref, band_ref, out_ref, turned_ref,
    incoming, arrived, turned_even, turned_odd, handed, products,
    left_high_even, left_high_odd, left_low_even, left_low_odd, right_high, right_low,
):
    turned = turned_even, turned_odd
    left_high, left_low = (left_high_even, left_high_odd), (left_low_even, left_low_odd)
    chunk, bands = incoming.shape[1:]
    chunks = band_ref.shape[0] // chunk
    groups = chunk // LANES
    stride = products.shape[0] // out_ref.shape[0]
    pairs = out_ref.shape[0]
    lines, blocks, window = shape
    count = pairs // SLICES
    width = bands // SLICES
    block = block_ref[0]

    def fetch(c):
        slot = lax.rem(c, 3)
        return pltpu.make_async_copy(
            band_ref.at[pl.ds(c * chunk, chunk), :], incoming.at[slot], arrived.at[slot]
        )

    def hand_on(c, parity):
        return pltpu.make_async_copy(turned[parity], turned_ref.at[c], handed.at[parity])

    def turn(c, parity, part):
        flat = turned[parity].reshape(bands * groups, LANES)
        for group in range(part, groups, SLICES):
            rows = pl.ds(group * LANES, LANES)
            flat[pl.ds(group, bands, stride=groups), :] = incoming[lax.rem(c, 3), rows, :].T

    def prepare(c, parity, part):
        here = pl.ds(part * width, width)
        right_high[:, here], right_low[:, here] = split(incoming[lax.rem(c, 3), :, here])
        for pair in range(part * count, part * count + count):
            per_share = pairs // (2 * lines)
            share, place = divmod(pair, per_share)
            index, step = pair_position(
                share * per_share * blocks + place, lines, blocks, window, occ_ref.shape[0]
            )
            index = index + block * step
            products[pl.ds(pair * stride, groups), :] = (
                turned[parity][occ_ref[index]] * turned[parity][vir_ref[index]]
            )
        for group in range(groups):
            weight = coulomb_ref[pl.ds(lax.rem(c, chunks) * groups + group, 1), :]
            value = products[pl.ds(part * count * stride + group, count, stride=stride), :]
            here = pl.ds(part * count, count)
            there = pl.ds(group * LANES, LANES)
            left_high[parity][here, there], left_low[parity][here, there] = split(value * weight)

    def multiply(parity, part):
        here = pl.ds(part * width, width)
        out_ref[:, here] += three_pass(
            left_high[parity][...], left_low[parity][...], right_high[:, here], right_low[:, here]
        )

    for c in range(min(3, chunks)):
        fetch(c).start()
    out_ref[...] = jnp.zeros_like(out_ref)
    fetch(0).wait()
    for part in range(SLICES):
        turn(0, 0, part)
    hand_on(0, 0).start()
    if chunks > 1:
        fetch(1).wait()
    for part in range(SLICES):
        if chunks > 1:
            turn(1, 1, part)
        prepare(0, 0, part)
    if chunks > 1:
        hand_on(1, 1).start()

    def advance(c, parity):
        @pl.when(c + 2 < chunks)
        def _():
            fetch(c + 2).wait()

        @pl.when(c + 3 < chunks)
        def _():
            fetch(c + 3).start()

        hand_on(c, parity).wait()
        for part in range(SLICES):
            multiply(parity, part)
            turn(c + 2, parity, part)
            prepare(c + 1, 1 - parity, part)

        @pl.when(c + 2 < chunks)
        def _():
            hand_on(c + 2, parity).start()

    @pl.loop(0, chunks // 2)
    def _(index):
        advance(2 * index, 0)
        advance(2 * index + 1, 1)

    if chunks % 2:
        advance(chunks - 1, 0)


def pair_coupling(band_vectors, coulomb, occ, vir, block, shape):
    basis_rows, bands = band_vectors.shape
    lines, blocks, window = shape
    pairs = occ.shape[0] // blocks
    chunk = math.gcd(CHUNK, basis_rows)
    groups = chunk // LANES
    stride = groups + 1 - groups % 2
    half = jnp.bfloat16
    scalars = pl.BlockSpec(memory_space=pltpu.SMEM)
    whole = pl.BlockSpec(memory_space=pltpu.VMEM)
    outside = pl.BlockSpec(memory_space=pl.ANY)
    return pl.pallas_call(
        functools.partial(coupling_kernel, shape),
        in_specs=[scalars] * 3 + [whole, outside],
        out_specs=[whole, outside],
        out_shape=[
            jax.ShapeDtypeStruct((pairs, bands), jnp.float32),
            jax.ShapeDtypeStruct((basis_rows // chunk, bands, groups, LANES), jnp.float32),
        ],
        scratch_shapes=[
            pltpu.VMEM((3, chunk, bands), jnp.float32),
            pltpu.SemaphoreType.DMA((3,)),
            pltpu.VMEM((bands, groups, LANES), jnp.float32),
            pltpu.VMEM((bands, groups, LANES), jnp.float32),
            pltpu.SemaphoreType.DMA((2,)),
            pltpu.VMEM((pairs * stride, LANES), jnp.float32),
        ]
        + [pltpu.VMEM((pairs, chunk), half)] * 4
        + [pltpu.VMEM((chunk, bands), half)] * 2,
        compiler_params=pltpu.CompilerParams(vmem_limit_bytes=VMEM_BYTES),
        cost_estimate=pl.CostEstimate(
            flops=6 * basis_rows * pairs * bands,
            bytes_accessed=8 * basis_rows * bands,
            transcendentals=0,
        ),
        name="coupling",
    )(block, occ, vir, coulomb.reshape(basis_rows // LANES, LANES), band_vectors)


def response_kernel(
    shape, half, block_ref, occ_ref, vir_ref, coulomb_ref, turned_ref, out_ref,
    turned, arrived, products, left_high_even, left_high_odd, left_low_even, left_low_odd,
    right_high, right_low,
):
    left_high, left_low = (left_high_even, left_high_odd), (left_low_even, left_low_odd)
    chunks, bands, groups, _ = turned_ref.shape
    pairs, own = out_ref.shape
    lines, blocks, window = shape
    height = left_high_even.shape[0]
    slices = pairs // height
    every = chunks * groups
    block = block_ref[0]
    inside, outside = window // (2 * lines * blocks), occ_ref.shape[0] - window
    outside = outside // (2 * lines * blocks)

    def fetch(c):
        here = pl.ds(pl.multiple_of(c * groups, groups), groups)
        return pltpu.make_async_copy(turned_ref.at[c], turned.at[:, here, :], arrived.at[c])

    def gather(index, place, here, stride):
        products[pl.ds(place * stride, here.size), :] = (
            turned[occ_ref[index], here, :] * turned[vir_ref[index], here, :]
        )

    def gather_slice(i, low, count, here, stride):
        core, line = lax.div(i, 2), lax.rem(i, 2) * (lines // 2)
        first = (line * 2 + core) * blocks + half * (blocks // 2)
        for pair in range(low, low + count):
            step, place = divmod(pair, blocks // 2 * (inside + outside))
            part, place = divmod(place, inside + outside)
            index = step * 2 * blocks + part
            if place < inside:
                index = first * inside + (index * inside + place)
            else:
                index = first * outside + (window + index * outside + place - inside)
            gather(index, pair, here, stride)

    def split_slice(parity, low, count, base, number, stride):
        for group in range(number):
            there = pl.ds(base + group * LANES, LANES)
            rows = pl.ds(low, count)
            left_high[parity][rows, there], left_low[parity][rows, there] = split(
                products[pl.ds(low * stride + group, count, stride=stride), :]
            )

    def multiply(i, parity, part):
        here = pl.ds(pl.multiple_of(i * height, height), height)
        depth = every * LANES // PIECES
        along = pl.ds(part * depth, depth)
        value = three_pass(
            left_high[parity][:, along], left_low[parity][:, along],
            right_high[along, :], right_low[along, :],
        )
        out_ref[here, :] = out_ref[here, :] + value if part else value

    for c in range(chunks):
        fetch(c).start()

    @pl.loop(0, chunks)
    def _(c):
        fetch(c).wait()
        here = pl.ds(pl.multiple_of(c * groups, groups), groups)
        base = pl.multiple_of(c * (groups * LANES), LANES)
        stride = groups + 1 - groups % 2
        for pair in range(own):
            share, place = divmod(pair, inside)
            gather(block * inside + (share * blocks * inside + place), pair, here, stride)
        for group in range(groups):
            weight = coulomb_ref[pl.ds(c * groups + group, 1), :]
            value = products[pl.ds(group, own, stride=stride), :] * weight
            there = pl.ds(base + group * LANES, LANES)
            right_high[there, :], right_low[there, :] = split(value.T)
        gather_slice(0, 0, height, here, stride)
        split_slice(0, 0, height, base, groups, stride)

    stride = every + 1 - every % 2
    count = height // PIECES

    def advance(i, parity, further):
        for part in range(PIECES):
            multiply(i, parity, part)
            if further:
                gather_slice(i + 1, part * count, count, pl.ds(0, every), stride)
                split_slice(1 - parity, part * count, count, 0, every, stride)

    @pl.loop(0, slices // 2 - 1)
    def _(index):
        advance(2 * index, 0, True)
        advance(2 * index + 1, 1, True)

    advance(slices - 2, 0, True)
    advance(slices - 1, 1, False)


def pair_response(turned, coulomb, occ, vir, block, shape, half):
    steps, bands, groups, _ = turned.shape
    lines, blocks, window = shape
    pairs = occ.shape[0]
    own = window // blocks
    every = steps * groups
    basis_rows = every * LANES
    height = pairs // PAIR_SLICES
    places = max(height * (every + 1 - every % 2), own * (groups + 1 - groups % 2))
    kind = jnp.bfloat16
    scalars = pl.BlockSpec(memory_space=pltpu.SMEM)
    whole = pl.BlockSpec(memory_space=pltpu.VMEM)
    return pl.pallas_call(
        functools.partial(response_kernel, shape, half),
        in_specs=[scalars] * 3 + [whole, pl.BlockSpec(memory_space=pl.ANY)],
        out_specs=whole,
        out_shape=jax.ShapeDtypeStruct((pairs // 2, own), jnp.float32),
        scratch_shapes=[
            pltpu.VMEM((bands, every, LANES), jnp.float32),
            pltpu.SemaphoreType.DMA((steps,)),
            pltpu.VMEM((places, LANES), jnp.float32),
        ]
        + [pltpu.VMEM((height, basis_rows), kind)] * 4
        + [pltpu.VMEM((basis_rows, own), kind)] * 2,
        compiler_params=pltpu.CompilerParams(vmem_limit_bytes=VMEM_BYTES),
        cost_estimate=pl.CostEstimate(
            flops=3 * basis_rows * pairs * own,
            bytes_accessed=4 * basis_rows * bands,
            transcendentals=0,
        ),
        name=f"response_{half}",
    )(block, occ, vir, coulomb.reshape(every, LANES), turned)


def per_device(band_vectors, coulomb, pair_weight, occ_index, vir_index, freq_index, freq_table):
    row_count = lax.axis_size("rows")
    col_count = lax.axis_size("cols")
    group_count = lax.axis_size("grp")
    blocks = col_count * group_count
    lines = row_count // 2
    row = lax.axis_index("rows")
    core, line = lax.rem(row, 2), lax.div(row, 2)
    column = lax.axis_index("cols")
    group = lax.axis_index("grp")
    block = group * col_count + column
    basis_rows, bands = band_vectors.shape
    pairs = occ_index.shape[0]
    window = PANEL * group_count
    basis = basis_rows * row_count

    def ordered(values):
        def shares(part):
            return part.reshape(lines, 2, blocks, -1).swapaxes(0, 1)

        return jnp.concatenate([shares(values[:window]), shares(values[window:])], axis=3)

    def own_window(values):
        shaped = values[:window].reshape(row_count, blocks, -1)
        return pick(shaped, block, 1).reshape(-1)

    def pick(values, index, axis=0):
        return lax.dynamic_index_in_dim(values, index, axis, keepdims=False)

    other_core = [(i, i ^ 1) for i in range(row_count)]

    def shift(step):
        return [(i, (i // 2 + step) % lines * 2 + i % 2) for i in range(row_count)]

    def add_cores(values):
        received = lax.ppermute(pick(values, 1 - core), "rows", other_core)
        return pick(values, core) + received

    def scatter_lines(values):
        arrived = [
            lax.ppermute(pick(values, lax.rem(line + step, lines)), "rows", shift(step))
            for step in range(1, lines)
        ]
        total = pick(values, line)
        for value in arrived:
            total = total + value
        return total

    def gather_blocks(values):
        across = [(i, i ^ 1) for i in range(col_count)]
        pair = jnp.stack([values, lax.ppermute(values, "cols", across)])
        pair = jnp.where(column == 0, pair, pair[::-1])
        across = [(i, i ^ 1) for i in range(group_count)]
        quad = jnp.stack([pair, lax.ppermute(pair, "grp", across)])
        quad = jnp.where(group == 0, quad, quad[::-1])
        return quad.reshape((blocks,) + values.shape)

    weights = ordered(pair_weight)
    shape = (lines, blocks, window)
    place = block.reshape(1)
    partial_coupling, turned = pair_coupling(
        band_vectors, coulomb, occ_index, vir_index, place, shape
    )
    share = pairs // row_count
    partial_coupling = add_cores(partial_coupling.reshape(2, lines, share // blocks, bands))
    partial_coupling, turned = lax.optimization_barrier((partial_coupling, turned))
    first = pair_response(turned, coulomb, occ_index, vir_index, place, shape, 0)
    coupling = scatter_lines(partial_coupling)
    first, coupling = lax.optimization_barrier((first, coupling))

    own_weights = pick(pick(weights, core), line)
    coupling = coupling * (pick(own_weights, block)[:, None] * (1.0 / math.sqrt(basis)))
    all_coupling = gather_blocks(coupling).reshape(share, bands)
    sub = window // (row_count * blocks)
    part = coupling[:sub]
    parts = [part] + [lax.ppermute(part, "rows", shift(step)) for step in range(1, lines)]

    def sum_cores(values):
        return add_cores(values.reshape(2, lines, share // 2, window // blocks))

    first = sum_cores(first)
    first, turned = lax.optimization_barrier((first, turned))
    second = pair_response(turned, coulomb, occ_index, vir_index, place, shape, 1)
    first = scatter_lines(first)
    second, first, all_coupling, *parts = lax.optimization_barrier(
        (second, first, all_coupling, *parts)
    )
    second = scatter_lines(sum_cores(second))
    response = jnp.concatenate([first, second]) * (
        own_weights.reshape(-1)[:, None] * own_window(pair_weight)[None, :] * (1.0 / basis)
    )

    parts = jnp.stack(parts)
    beside = lax.ppermute(parts, "rows", other_core)
    both = jnp.where(core == 0, jnp.stack([parts, beside], 1), jnp.stack([beside, parts], 1))
    both = jnp.roll(both[::-1], line + 1, axis=0)
    window_coupling = both.reshape(row_count * sub, bands)
    matches = freq_index[:, None] == jnp.arange(freq_table.shape[0], dtype=jnp.int32)[None, :]
    band_weight = jnp.sum(jnp.where(matches, freq_table[None, :], 0.0), axis=1)
    mixed = lax.dot_general(
        all_coupling, response, (((0,), (0,)), ((), ())),
        precision=lax.Precision.HIGH, preferred_element_type=jnp.float32,
    )
    mixed = add_cores(mixed.reshape(lines, 2, bands // row_count, -1).swapaxes(0, 1))
    mixed = scatter_lines(mixed)
    energy = lax.dot_general(
        mixed, window_coupling, (((1,), (0,)), ((), ())),
        precision=lax.Precision.HIGH, preferred_element_type=jnp.float32,
    )
    here = bands // row_count
    own_band_weight = lax.dynamic_slice_in_dim(band_weight, row * here, here, 0)
    energy = energy * (
        own_band_weight[:, None] * band_weight[None, :] * (1.0 / math.sqrt(window))
    )
    energy = energy.reshape(col_count, here // col_count, group_count, bands // group_count)
    total = pick(pick(energy, column), group, 1)
    for step in range(1, blocks):
        there_group, there_column = divmod(step, col_count)
        away_group = lax.rem(group + there_group, group_count)
        away_column = lax.rem(column + there_column, col_count)
        targets = [
            (
                i,
                (i // col_count + there_group) % group_count * col_count
                + (i % col_count + there_column) % col_count,
            )
            for i in range(blocks)
        ]
        total = total + lax.ppermute(
            pick(pick(energy, away_column), away_group, 1), ("grp", "cols"), targets
        )
    return total


def solution(mesh):
    placed = (P("rows", None), P("rows"), P(), P(), P(), P(), P())
    return jax.shard_map(
        per_device,
        mesh=mesh,
        in_specs=placed,
        out_specs=P(("rows", "cols"), "grp"),
        check_vma=False,
    )
```

```python
import functools
import math

import jax
import jax.numpy as jnp
from jax import lax
from jax.experimental import pallas as pl
from jax.experimental.pallas import tpu as pltpu
from jax.sharding import PartitionSpec as P

PANEL = 512
LANES = 128
CHUNK = 1024
SLICES = 4
PAIR_SLICES = 8
VMEM_BYTES = 60 * 2**20


def split(value):
    high = value.astype(jnp.bfloat16)
    return high, (value - high.astype(jnp.float32)).astype(jnp.bfloat16)


def three_pass(left_high, left_low, right_high, right_low):
    def dot(left, right):
        return jnp.dot(left, right, preferred_element_type=jnp.float32)

    return dot(left_high, right_high) + (dot(left_low, right_high) + dot(left_high, right_low))


def pair_position(place, lines, blocks, window, pairs):
    inside, outside = window // (2 * lines * blocks), (pairs - window) // (2 * lines * blocks)
    rest, place = divmod(place, inside + outside)
    rest, block = divmod(rest, blocks)
    core, line = divmod(rest, lines)
    share = (line * 2 + core) * blocks + block
    if place < inside:
        return share * inside + place, inside
    return window + share * outside + place - inside, outside


def coupling_kernel(
    shape, block_ref, occ_ref, vir_ref, coulomb_ref, band_ref, out_ref, turned_ref,
    incoming, arrived, turned_even, turned_odd, handed, products,
    left_high_even, left_high_odd, left_low_even, left_low_odd, right_high, right_low,
):
    turned = turned_even, turned_odd
    left_high, left_low = (left_high_even, left_high_odd), (left_low_even, left_low_odd)
    chunk, bands = incoming.shape[1:]
    chunks = band_ref.shape[0] // chunk
    groups = chunk // LANES
    stride = products.shape[0] // out_ref.shape[0]
    pairs = out_ref.shape[0]
    lines, blocks, window = shape
    count = pairs // SLICES
    width = bands // SLICES
    block = block_ref[0]

    def fetch(c):
        slot = lax.rem(c, 3)
        return pltpu.make_async_copy(
            band_ref.at[pl.ds(c * chunk, chunk), :], incoming.at[slot], arrived.at[slot]
        )

    def hand_on(c, parity):
        return pltpu.make_async_copy(turned[parity], turned_ref.at[c], handed.at[parity])

    def turn(c, parity, part):
        flat = turned[parity].reshape(bands * groups, LANES)
        for group in range(part, groups, SLICES):
            rows = pl.ds(group * LANES, LANES)
            flat[pl.ds(group, bands, stride=groups), :] = incoming[lax.rem(c, 3), rows, :].T

    def prepare(c, parity, part):
        here = pl.ds(part * width, width)
        right_high[:, here], right_low[:, here] = split(incoming[lax.rem(c, 3), :, here])
        for pair in range(part * count, part * count + count):
            per_share = pairs // (2 * lines)
            share, place = divmod(pair, per_share)
            index, step = pair_position(
                share * per_share * blocks + place, lines, blocks, window, occ_ref.shape[0]
            )
            index = index + block * step
            products[pl.ds(pair * stride, groups), :] = (
                turned[parity][occ_ref[index]] * turned[parity][vir_ref[index]]
            )
        for group in range(groups):
            weight = coulomb_ref[pl.ds(lax.rem(c, chunks) * groups + group, 1), :]
            value = products[pl.ds(part * count * stride + group, count, stride=stride), :]
            here = pl.ds(part * count, count)
            there = pl.ds(group * LANES, LANES)
            left_high[parity][here, there], left_low[parity][here, there] = split(value * weight)

    def multiply(parity, part):
        here = pl.ds(part * width, width)
        out_ref[:, here] += three_pass(
            left_high[parity][...], left_low[parity][...], right_high[:, here], right_low[:, here]
        )

    for c in range(min(3, chunks)):
        fetch(c).start()
    out_ref[...] = jnp.zeros_like(out_ref)
    fetch(0).wait()
    for part in range(SLICES):
        turn(0, 0, part)
    hand_on(0, 0).start()
    if chunks > 1:
        fetch(1).wait()
    for part in range(SLICES):
        if chunks > 1:
            turn(1, 1, part)
        prepare(0, 0, part)
    if chunks > 1:
        hand_on(1, 1).start()

    def advance(c, parity):
        @pl.when(c + 2 < chunks)
        def _():
            fetch(c + 2).wait()

        @pl.when(c + 3 < chunks)
        def _():
            fetch(c + 3).start()

        hand_on(c, parity).wait()
        for part in range(SLICES):
            multiply(parity, part)
            turn(c + 2, parity, part)
            prepare(c + 1, 1 - parity, part)

        @pl.when(c + 2 < chunks)
        def _():
            hand_on(c + 2, parity).start()

    @pl.loop(0, chunks // 2)
    def _(index):
        advance(2 * index, 0)
        advance(2 * index + 1, 1)

    if chunks % 2:
        advance(chunks - 1, 0)


def pair_coupling(band_vectors, coulomb, occ, vir, block, shape):
    basis_rows, bands = band_vectors.shape
    lines, blocks, window = shape
    pairs = occ.shape[0] // blocks
    chunk = math.gcd(CHUNK, basis_rows)
    groups = chunk // LANES
    stride = groups + 1 - groups % 2
    half = jnp.bfloat16
    scalars = pl.BlockSpec(memory_space=pltpu.SMEM)
    whole = pl.BlockSpec(memory_space=pltpu.VMEM)
    outside = pl.BlockSpec(memory_space=pl.ANY)
    return pl.pallas_call(
        functools.partial(coupling_kernel, shape),
        in_specs=[scalars] * 3 + [whole, outside],
        out_specs=[whole, outside],
        out_shape=[
            jax.ShapeDtypeStruct((pairs, bands), jnp.float32),
            jax.ShapeDtypeStruct((basis_rows // chunk, bands, groups, LANES), jnp.float32),
        ],
        scratch_shapes=[
            pltpu.VMEM((3, chunk, bands), jnp.float32),
            pltpu.SemaphoreType.DMA((3,)),
            pltpu.VMEM((bands, groups, LANES), jnp.float32),
            pltpu.VMEM((bands, groups, LANES), jnp.float32),
            pltpu.SemaphoreType.DMA((2,)),
            pltpu.VMEM((pairs * stride, LANES), jnp.float32),
        ]
        + [pltpu.VMEM((pairs, chunk), half)] * 4
        + [pltpu.VMEM((chunk, bands), half)] * 2,
        compiler_params=pltpu.CompilerParams(vmem_limit_bytes=VMEM_BYTES),
        cost_estimate=pl.CostEstimate(
            flops=6 * basis_rows * pairs * bands,
            bytes_accessed=8 * basis_rows * bands,
            transcendentals=0,
        ),
        name="coupling",
    )(block, occ, vir, coulomb.reshape(basis_rows // LANES, LANES), band_vectors)


def response_kernel(
    shape, block_ref, occ_ref, vir_ref, coulomb_ref, turned_ref, out_ref,
    turned, arrived, products, left_high_even, left_high_odd, left_low_even, left_low_odd,
    right_high, right_low,
):
    left_high, left_low = (left_high_even, left_high_odd), (left_low_even, left_low_odd)
    chunks, bands, groups, _ = turned_ref.shape
    pairs, own = out_ref.shape
    lines, blocks, window = shape
    height = left_high_even.shape[0]
    slices = pairs // height
    every = chunks * groups
    block = block_ref[0]
    inside, outside = window // (2 * lines * blocks), (pairs - window) // (2 * lines * blocks)
    half_slices = slices // 2
    per_slice = lines // half_slices

    def fetch(c):
        here = pl.ds(pl.multiple_of(c * groups, groups), groups)
        return pltpu.make_async_copy(turned_ref.at[c], turned.at[:, here, :], arrived.at[c])

    def gather(index, place, here, stride):
        products[pl.ds(place * stride, here.size), :] = (
            turned[occ_ref[index], here, :] * turned[vir_ref[index], here, :]
        )

    def gather_slice(i, here, stride):
        first = (lax.rem(i, half_slices) * (per_slice * 2) + lax.div(i, half_slices)) * blocks
        for pair in range(height):
            share, place = divmod(pair, blocks * (inside + outside))
            part, place = divmod(place, inside + outside)
            index = share * 2 * blocks + part
            if place < inside:
                index = first * inside + (index * inside + place)
            else:
                index = first * outside + (window + index * outside + place - inside)
            gather(index, pair, here, stride)

    def split_slice(parity, base, count, stride):
        for group in range(count):
            there = pl.ds(base + group * LANES, LANES)
            left_high[parity][:, there], left_low[parity][:, there] = split(
                products[pl.ds(group, height, stride=stride), :]
            )

    def multiply(i, parity):
        here = pl.ds(pl.multiple_of(i * height, height), height)
        out_ref[here, :] = three_pass(
            left_high[parity][...], left_low[parity][...], right_high[...], right_low[...]
        )

    for c in range(chunks):
        fetch(c).start()
    out_ref[pl.ds(0, height), :] = jnp.zeros((height, own), jnp.float32)

    @pl.loop(0, chunks)
    def _(c):
        fetch(c).wait()
        here = pl.ds(pl.multiple_of(c * groups, groups), groups)
        base = pl.multiple_of(c * (groups * LANES), LANES)
        stride = groups + 1 - groups % 2
        for pair in range(own):
            share, place = divmod(pair, inside)
            gather(block * inside + (share * blocks * inside + place), pair, here, stride)
        for group in range(groups):
            weight = coulomb_ref[pl.ds(c * groups + group, 1), :]
            value = products[pl.ds(group, own, stride=stride), :] * weight
            there = pl.ds(base + group * LANES, LANES)
            right_high[there, :], right_low[there, :] = split(value.T)
        gather_slice(0, here, stride)
        split_slice(0, base, groups, stride)
        along = pl.ds(base, groups * LANES)
        out_ref[pl.ds(0, height), :] += three_pass(
            left_high[0][:, along], left_low[0][:, along], right_high[along, :], right_low[along, :]
        )

    stride = every + 1 - every % 2

    def gather_whole(i, parity):
        gather_slice(i, pl.ds(0, every), stride)
        split_slice(parity, 0, every, stride)

    gather_whole(1, 1)

    @pl.loop(0, slices // 2 - 1)
    def _(index):
        for parity in (1, 0):
            i = 2 * index + 2 - parity
            multiply(i, parity)
            gather_whole(i + 1, 1 - parity)

    multiply(slices - 1, 1)


def pair_response(turned, coulomb, occ, vir, block, shape):
    steps, bands, groups, _ = turned.shape
    lines, blocks, window = shape
    pairs = occ.shape[0]
    own = window // blocks
    every = steps * groups
    basis_rows = every * LANES
    height = pairs // PAIR_SLICES
    places = max(height * (every + 1 - every % 2), own * (groups + 1 - groups % 2))
    half = jnp.bfloat16
    scalars = pl.BlockSpec(memory_space=pltpu.SMEM)
    whole = pl.BlockSpec(memory_space=pltpu.VMEM)
    return pl.pallas_call(
        functools.partial(response_kernel, shape),
        in_specs=[scalars] * 3 + [whole, pl.BlockSpec(memory_space=pl.ANY)],
        out_specs=whole,
        out_shape=jax.ShapeDtypeStruct((pairs, own), jnp.float32),
        scratch_shapes=[
            pltpu.VMEM((bands, every, LANES), jnp.float32),
            pltpu.SemaphoreType.DMA((steps,)),
            pltpu.VMEM((places, LANES), jnp.float32),
        ]
        + [pltpu.VMEM((height, basis_rows), half)] * 4
        + [pltpu.VMEM((basis_rows, own), half)] * 2,
        compiler_params=pltpu.CompilerParams(vmem_limit_bytes=VMEM_BYTES),
        cost_estimate=pl.CostEstimate(
            flops=6 * basis_rows * pairs * own,
            bytes_accessed=4 * basis_rows * bands,
            transcendentals=0,
        ),
        name="response",
    )(block, occ, vir, coulomb.reshape(basis_rows // LANES, LANES), turned)


def per_device(band_vectors, coulomb, pair_weight, occ_index, vir_index, freq_index, freq_table):
    row_count = lax.axis_size("rows")
    col_count = lax.axis_size("cols")
    group_count = lax.axis_size("grp")
    blocks = col_count * group_count
    lines = row_count // 2
    row = lax.axis_index("rows")
    core, line = lax.rem(row, 2), lax.div(row, 2)
    column = lax.axis_index("cols")
    group = lax.axis_index("grp")
    block = group * col_count + column
    basis_rows, bands = band_vectors.shape
    pairs = occ_index.shape[0]
    window = PANEL * group_count
    basis = basis_rows * row_count

    def ordered(values):
        def shares(part):
            return part.reshape(lines, 2, blocks, -1).swapaxes(0, 1)

        return jnp.concatenate([shares(values[:window]), shares(values[window:])], axis=3)

    def own_window(values):
        shaped = values[:window].reshape(row_count, blocks, -1)
        return pick(shaped, block, 1).reshape(-1)

    def pick(values, index, axis=0):
        return lax.dynamic_index_in_dim(values, index, axis, keepdims=False)

    other_core = [(i, i ^ 1) for i in range(row_count)]

    def shift(step):
        return [(i, (i // 2 + step) % lines * 2 + i % 2) for i in range(row_count)]

    def add_cores(values):
        received = lax.ppermute(pick(values, 1 - core), "rows", other_core)
        return pick(values, core) + received

    def scatter_lines(values):
        arrived = [
            lax.ppermute(pick(values, lax.rem(line + step, lines)), "rows", shift(step))
            for step in range(1, lines)
        ]
        total = pick(values, line)
        for value in arrived:
            total = total + value
        return total

    def gather_blocks(values):
        across = [(i, i ^ 1) for i in range(col_count)]
        pair = jnp.stack([values, lax.ppermute(values, "cols", across)])
        pair = jnp.where(column == 0, pair, pair[::-1])
        across = [(i, i ^ 1) for i in range(group_count)]
        quad = jnp.stack([pair, lax.ppermute(pair, "grp", across)])
        quad = jnp.where(group == 0, quad, quad[::-1])
        return quad.reshape((blocks,) + values.shape)

    weights = ordered(pair_weight)
    shape = (lines, blocks, window)
    place = block.reshape(1)
    partial_coupling, turned = pair_coupling(
        band_vectors, coulomb, occ_index, vir_index, place, shape
    )
    share = pairs // row_count
    partial_coupling = add_cores(partial_coupling.reshape(2, lines, share // blocks, bands))
    partial_coupling, turned = lax.optimization_barrier((partial_coupling, turned))
    partial_response = pair_response(turned, coulomb, occ_index, vir_index, place, shape)
    coupling = scatter_lines(partial_coupling)
    partial_response, coupling = lax.optimization_barrier((partial_response, coupling))
    partial_response = add_cores(partial_response.reshape(2, lines, share, window // blocks))
    partial_response, coupling = lax.optimization_barrier((partial_response, coupling))
    own_weights = pick(pick(weights, core), line)
    coupling = coupling * (pick(own_weights, block)[:, None] * (1.0 / math.sqrt(basis)))
    all_coupling = gather_blocks(coupling).reshape(share, bands)
    response = scatter_lines(partial_response)
    response = response * (
        own_weights.reshape(-1)[:, None] * own_window(pair_weight)[None, :] * (1.0 / basis)
    )
    sub = window // (row_count * blocks)
    response, all_coupling, part = lax.optimization_barrier(
        (response, all_coupling, coupling[:sub])
    )
    parts = [part] + [lax.ppermute(part, "rows", shift(step)) for step in range(1, lines)]
    mixed = lax.dot_general(
        all_coupling, response, (((0,), (0,)), ((), ())),
        precision=lax.Precision.HIGH, preferred_element_type=jnp.float32,
    )
    mixed = add_cores(mixed.reshape(lines, 2, bands // row_count, -1).swapaxes(0, 1))
    mixed = scatter_lines(mixed)
    order = lax.rem(line - jnp.arange(lines) + lines, lines)
    parts = jnp.stack(parts)[order]
    beside = lax.ppermute(parts, "rows", other_core)
    pairs_of = jnp.where(core == 0, jnp.stack([parts, beside], 1), jnp.stack([beside, parts], 1))
    window_coupling = pairs_of.reshape(row_count * sub, bands)
    matches = freq_index[:, None] == jnp.arange(freq_table.shape[0], dtype=jnp.int32)[None, :]
    band_weight = jnp.sum(jnp.where(matches, freq_table[None, :], 0.0), axis=1)
    energy = lax.dot_general(
        mixed, window_coupling, (((1,), (0,)), ((), ())),
        precision=lax.Precision.HIGH, preferred_element_type=jnp.float32,
    )
    here = bands // row_count
    own_band_weight = lax.dynamic_slice_in_dim(band_weight, row * here, here, 0)
    energy = energy * (
        own_band_weight[:, None] * band_weight[None, :] * (1.0 / math.sqrt(window))
    )
    energy = energy.reshape(col_count, here // col_count, group_count, bands // group_count)
    total = pick(pick(energy, column), group, 1)
    for step in range(1, blocks):
        there_group, there_column = divmod(step, col_count)
        away_group = lax.rem(group + there_group, group_count)
        away_column = lax.rem(column + there_column, col_count)
        targets = [
            (
                i,
                (i // col_count + there_group) % group_count * col_count
                + (i % col_count + there_column) % col_count,
            )
            for i in range(blocks)
        ]
        total = total + lax.ppermute(
            pick(pick(energy, away_column), away_group, 1), ("grp", "cols"), targets
        )
    return total


def solution(mesh):
    placed = (P("rows", None), P("rows"), P(), P(), P(), P(), P())
    return jax.shard_map(
        per_device,
        mesh=mesh,
        in_specs=placed,
        out_specs=P(("rows", "cols"), "grp"),
        check_vma=False,
    )
```
